128 devices in a mesh: dp: 4 (over z), expert: 32 (over y, x, core).
Axes of the slice: x: 4, y: 4, z: 4, core: 2. Of those that a mesh axis runs over, the one named last changes fastest.
Arguments:
- tokens: bfloat16 [32768, 4096], P(('dp', 'expert')), may hold values from -6 to 6
- grad_out: bfloat16 [32768, 4096], P(('dp', 'expert')), may hold values from -6 to 6
- expert_ids: int32 [32768, 2], P(('dp', 'expert')), may hold values from 0 to 31, all different within a row; in each aligned block of 256 rows (0 to 255, 256 to 511, ...) at most 24 rows name the same one
- combine: bfloat16 [32768, 2], P(('dp', 'expert')), may hold values from 0.099609375 to 1
- w_gate: bfloat16 [32, 4096, 512], P('expert'), may hold values from -0.09375 to 0.09375
- w_up: bfloat16 [32, 4096, 512], P('expert'), may hold values from -0.09375 to 0.09375
- w_down: bfloat16 [32, 512, 4096], P('expert'), may hold values from -0.25 to 0.25
Outputs:
- grad_tokens: bfloat16 [32768, 4096], P(('dp', 'expert'))
- grad_combine: bfloat16 [32768, 2], P(('dp', 'expert'))
- grad_gate: bfloat16 [32, 4096, 512], P('expert', 'dp')
- grad_up: bfloat16 [32, 4096, 512], P('expert', 'dp')
- grad_down: bfloat16 [32, 512, 4096], P('expert', None, 'dp')
The draws below stay inside these ranges and needn't reach their ends.
Inputs may be any that keep to these rules, and one draw needn't show every extreme that they name: `expert_ids`: the two experts of a token differ. In each aligned block of 256 rows (the rows of one device) no expert is named more than 24 times, a bound that some block reaches.
All inputs are finite; a program needn't handle non-finite values.
Results may differ from the reference program's by a relative error of at most 0.011.
Values may be sent and summed in bfloat16 or wider, within the bound.
A program may use at most 192 MiB of HBM per device.

```python
import math
import jax
import jax.numpy as jnp
import numpy as np
from jax import lax

D = 4096
HID = 512
TOK_DEV = 256
TOKENS = 32768
EXPERTS = 32
CAP = 24
DEVICES = 128


def levels(own_key, extent, pieces, smallest, largest):
    def one(axis_at, blocks):
        heights = jax.random.uniform(jax.random.fold_in(jax.random.fold_in(own_key, 6), axis_at), (blocks,), jnp.float32, smallest / len(pieces), largest / len(pieces))
        return jnp.repeat(jnp.exp(heights), extent[axis_at] // blocks).reshape((-1,) + (1,) * (len(extent) - axis_at - 1))

    level = one(*pieces[0])
    for cut in pieces[1:]:
        level = level * one(*cut)
    return level


def shared_out(own_key, own, number, rows, count, top, reach, slope):
    ranking = jax.random.permutation(own_key, count)
    packed, usual = portions_of(count, rows * top, reach, slope, True), portions_of(count, rows * top, reach, slope, False)
    places = jnp.arange(count)

    def named(tallies, turn):
        used = int((tallies > 0).sum())
        fixed = max(1, used // 4)
        moved = fixed + (places - fixed + turn * (used - fixed)) % max(1, count - fixed)
        return jnp.zeros((count,), jnp.int32).at[ranking[jnp.where(places < fixed, places, moved)]].set(jnp.asarray(tallies, jnp.int32))

    tallies = jnp.where(number % 4 == 0, named(packed, number // 4), named(usual, number - number // 4 - 1))
    mixed = jax.random.permutation(jax.random.fold_in(own, 3), count)
    giver, sink = mixed[0:count // 2 * 2:2], mixed[1:count // 2 * 2:2]
    slack = jnp.minimum(tallies[giver] - 1, reach - tallies[sink]) // 2
    slack = jnp.where((giver == ranking[0]) | (sink == ranking[0]) | (tallies[sink] == 0), 0, jnp.maximum(slack, 0))
    moved = jax.random.randint(jax.random.fold_in(own, 4), (count // 2,), 0, 1 << 20) % (slack + 1)
    tallies = tallies.at[giver].add(-moved).at[sink].add(moved)
    items = jnp.searchsorted(jnp.cumsum(tallies), jnp.arange(rows * top), side="right").astype(jnp.int32)
    grid = items.reshape(top, rows).T
    grid = grid[jax.random.permutation(jax.random.fold_in(own, 1), rows)]
    turn = jax.random.randint(jax.random.fold_in(own, 2), (rows, 1), 0, top)
    return jnp.take_along_axis(grid, (jnp.arange(top)[None, :] + turn) % top, axis=1)


def portions_of(number_of, total, most, lean, full):
    loads = [(1 << 20) // math.isqrt(grade ** lean) + 1 for grade in range(1, number_of + 1)]
    largest = most if full else min(most, max(-(-total // number_of), total * loads[0] // sum(loads)))
    least = 1 if total - largest >= number_of - 1 else 0
    holding, surplus = [largest] + [least] * (number_of - 1), total - largest - least * (number_of - 1)
    while surplus > 0:
        movable = [i for i in range(1, number_of) if holding[i] < largest] or [i for i in range(1, number_of) if holding[i] < most]
        mass, remaining = sum([loads[i] for i in movable]), surplus
        for i in movable:
            more = min(most - holding[i], max(1, remaining * loads[i] // mass), surplus)
            holding[i] = holding[i] + more
            surplus = surplus - more
    return np.array(holding)


def scatter_about(stream_key, shape, deviation, limit, shards=(), kind=jnp.bfloat16):
    result = deviation * jax.random.normal(stream_key, shape, jnp.float32)
    if shards:
        result = result * levels(stream_key, shape, shards, -0.22, 0.18)
    return jnp.clip(result, -limit, limit).astype(kind)


def setup_inputs(seed: int = 0) -> dict:
    splits = jax.random.split(jax.random.key(seed), 8)
    tokens = scatter_about(splits[0], (TOKENS, D), 1.0, 6.0, ((0, 128),))
    grad_out = scatter_about(splits[1], (TOKENS, D), 1.0, 6.0, ((0, 128),))
    expert_ids_keys = jax.random.split(jax.random.fold_in(splits[2], 1), TOKENS // TOK_DEV)
    expert_ids_turns = jax.random.permutation(jax.random.fold_in(splits[2], 3), TOKENS // TOK_DEV)
    expert_ids = jax.vmap(lambda own, number: shared_out(jax.random.fold_in(splits[2], 2), own, number, TOK_DEV, EXPERTS, 2, CAP, 2))(expert_ids_keys, expert_ids_turns).reshape((TOKENS, 2))
    combine = jnp.clip(0.099609375 + 0.9003906 * jax.random.uniform(splits[3], (TOKENS, 2), jnp.float32) ** levels(splits[3], (TOKENS, 2), ((0, 128),), -0.2, 0.2), 0.099609375, 1.0).astype(jnp.bfloat16)
    w_gate = scatter_about(splits[4], (EXPERTS, D, HID), D ** -0.5, 0.09375, ((0, 32),))
    w_up = scatter_about(splits[5], (EXPERTS, D, HID), D ** -0.5, 0.09375, ((0, 32),))
    w_down = scatter_about(splits[6], (EXPERTS, HID, D), HID ** -0.5, 0.25, ((0, 32),))
    return {"tokens": tokens, "grad_out": grad_out, "expert_ids": expert_ids, "combine": combine, "w_gate": w_gate, "w_up": w_up, "w_down": w_down}


def contract(left, right, left_dim, right_dim):
    return lax.dot_general(left, right, (((left_dim,), (right_dim,)), ((), ())), preferred_element_type=jnp.float32)


def block_places(block_ids):
    flat_ids = block_ids.reshape(-1).astype(jnp.int32)
    labels = jnp.arange(EXPERTS, dtype=jnp.int32)
    hits = (flat_ids[:, None] == labels[None, :]).astype(jnp.int32)
    earlier = jnp.cumsum(hits, axis=0) - hits
    slot = jnp.sum(earlier * hits, axis=1)
    return (flat_ids * CAP + slot).astype(jnp.int32)


def expert_backward(rows_x, rows_dy, rows_p, gate_w, up_w, down_w):
    gate = jnp.dot(rows_x, gate_w, preferred_element_type=jnp.float32)
    upper = jnp.dot(rows_x, up_w, preferred_element_type=jnp.float32)
    sigma = jax.nn.sigmoid(gate)
    swish = gate * sigma
    hidden = (swish * upper).astype(jnp.bfloat16)
    hidden_grad = contract(rows_dy, down_w, 1, 1)
    combine_grad = jnp.sum(hidden.astype(jnp.float32) * hidden_grad, axis=1).astype(jnp.bfloat16)
    weight = rows_p.astype(jnp.float32)[:, None]
    scaled_grad = weight * hidden_grad
    gate_grad = (scaled_grad * upper * sigma * (1.0 + gate * (1.0 - sigma))).astype(jnp.bfloat16)
    up_grad = (scaled_grad * swish).astype(jnp.bfloat16)
    scaled_hidden = (weight * hidden.astype(jnp.float32)).astype(jnp.bfloat16)
    pick_grad = (contract(gate_grad, gate_w, 1, 1) + contract(up_grad, up_w, 1, 1)).astype(jnp.bfloat16)
    return pick_grad, combine_grad, gate_grad, up_grad, scaled_hidden


def reference(tokens, grad_out, expert_ids, combine, w_gate, w_up, w_down):
    blocks = expert_ids.reshape(DEVICES, TOK_DEV, 2)
    local = jax.vmap(block_places)(blocks)
    device_row = jnp.arange(DEVICES, dtype=jnp.int32)[:, None]
    spread = ((local // CAP) * (DEVICES * CAP) + device_row * CAP + local % CAP).astype(jnp.int32)
    picks = 2 * TOKENS
    filler = jnp.full((EXPERTS * DEVICES * CAP,), picks, jnp.int32)
    filler = filler.at[spread.reshape(-1)].set(jnp.arange(picks, dtype=jnp.int32))
    filler = filler.reshape(EXPERTS, DEVICES * CAP)
    zero_row = jnp.zeros((1, D), jnp.bfloat16)
    tokens_ext = jnp.concatenate([tokens, zero_row], axis=0)
    grads_ext = jnp.concatenate([grad_out, zero_row], axis=0)
    weights_ext = jnp.concatenate([combine.reshape(-1), jnp.zeros((1,), jnp.bfloat16)], axis=0)

    def step(carry, items):
        pick_store, combine_store = carry
        index_row, gate_w, up_w, down_w = items
        owner = (index_row // 2).astype(jnp.int32)
        rows_x = tokens_ext[owner]
        rows_dy = grads_ext[owner]
        outs = expert_backward(rows_x, rows_dy, weights_ext[index_row], gate_w, up_w, down_w)
        pick_grad, combine_grad, gate_grad, up_grad, scaled_hidden = outs
        pick_store = pick_store.at[index_row].set(pick_grad)
        combine_store = combine_store.at[index_row].set(combine_grad)
        gate_sum = contract(rows_x, gate_grad, 0, 0).astype(jnp.bfloat16)
        up_sum = contract(rows_x, up_grad, 0, 0).astype(jnp.bfloat16)
        down_sum = contract(scaled_hidden, rows_dy, 0, 0).astype(jnp.bfloat16)
        return (pick_store, combine_store), (gate_sum, up_sum, down_sum)

    start = (jnp.zeros((picks + 1, D), jnp.bfloat16), jnp.zeros((picks + 1,), jnp.bfloat16))
    (pick_store, combine_store), (grad_gate, grad_up, grad_down) = lax.scan(step, start, (filler, w_gate, w_up, w_down))
    pairs = pick_store[:picks].astype(jnp.float32).reshape(TOKENS, 2, D)
    grad_tokens = jnp.sum(pairs, axis=1).astype(jnp.bfloat16)
    grad_combine = combine_store[:picks].reshape(TOKENS, 2)
    return grad_tokens, grad_combine, grad_gate, grad_up, grad_down
```

```python
import functools

import jax
import jax.numpy as jnp
from jax import lax
from jax.experimental import pallas as pl
from jax.experimental.pallas import tpu as pltpu
from jax.sharding import PartitionSpec as P

MESH = pl.DeviceIdType.MESH
NX, NY, NZ, NE = 4, 4, 4, 32
CAP = 24
D, HID = 4096, 512
SLICE = D // NZ
GROUP = 8
GROUPS = NE // GROUP
ROWS = GROUP * CAP
OFFSETS = (
    (1, 0), (3, 0), (0, 1), (0, 3), (1, 1), (3, 3), (1, 3), (3, 1),
    (2, 0), (0, 2), (1, 2), (3, 2), (2, 1), (2, 3), (2, 2),
)


def offset(i, core):
    dx, dy = OFFSETS[i]
    return dx + core * (dy - dx), dy + core * (dx - dy)


def expert_at(x, y, core):
    return (y % NY) * (2 * NX) + (x % NX) * 2 + core


def nt(left, right):
    return lax.dot_general(left, right, (((1,), (1,)), ((), ())), preferred_element_type=jnp.float32)


def tn(left, right):
    return lax.dot_general(left, right, (((0,), (0,)), ((), ())), preferred_element_type=jnp.float32)


def kernel(
    sx, sdy, wg_h, wu_h, wd_h,
    back, back_c, out_g, out_u, out_d,
    xr, dyr, pg, pc, wg, wu, wd, xz, gz, gown, hid, dn_out, dn_in, fa, fb,
    w_sem, loc_sem, x_recv, dy_recv, x_send, dy_send, pg_recv, pg_send, pc_recv, pc_send,
    xz_recv, xz_send, gz_recv, gz_send, dn_recv, dn_send,
):
    z = lax.axis_index("dp")
    ex = lax.axis_index("expert")
    c = ex % 2
    x = (ex // 2) % NX
    y = ex // (2 * NX)

    loads = [
        pltpu.make_async_copy(wg_h, wg, w_sem.at[0]),
        pltpu.make_async_copy(wu_h, wu, w_sem.at[1]),
        pltpu.make_async_copy(wd_h, wd, w_sem.at[2]),
        pltpu.make_async_copy(sx.at[ex], xr.at[0], loc_sem.at[0]),
        pltpu.make_async_copy(sdy.at[ex], dyr.at[0], loc_sem.at[1]),
    ]

    barrier = pltpu.get_barrier_semaphore()

    def greet(k, carry):
        pl.semaphore_signal(barrier, inc=1, device_id=(z, (ex + k) % NE), device_id_type=MESH)
        return carry

    lax.fori_loop(1, NE, greet, 0)
    for j in range(1, NZ):
        pl.semaphore_signal(barrier, inc=1, device_id=((z + j) % NZ, ex), device_id_type=MESH)
    for load in loads:
        load.start()
    pl.semaphore_wait(barrier, NE - 1 + NZ - 1)

    def to_expert(src, dst, send, recv, i, core):
        if i < 0:
            to, slot = ex + 1 - 2 * c, 1
            group = 0
        else:
            dx, dy = offset(i, c)
            to, slot = expert_at(x + dx, y + dy, core), 2 + 2 * i + c
            group = (2 + 2 * i) // GROUP
        return pltpu.make_async_remote_copy(
            src_ref=src.at[to], dst_ref=dst.at[slot], send_sem=send, recv_sem=recv.at[group],
            device_id=(z, to), device_id_type=MESH,
        )

    for g in range(GROUPS):
        for src, dst, send, recv in ((sx, xr, x_send, x_recv), (sdy, dyr, dy_send, dy_recv)):
            for slot in range(GROUP * g, GROUP * (g + 1), 2):
                if slot == 0:
                    to_expert(src, dst, send, recv, -1, 0).start()
                else:
                    for core in range(2):
                        to_expert(src, dst, send, recv, (slot - 2) // 2, core).start()

    def wait_recv(dst, sem):
        pltpu.make_async_remote_copy(
            src_ref=dst, dst_ref=dst, send_sem=x_send, recv_sem=sem,
            device_id=(z, (ex + 1) % NE), device_id_type=MESH,
        ).wait_recv()

    def wait_send(src, sem):
        pltpu.make_async_remote_copy(
            src_ref=src, dst_ref=src, send_sem=sem, recv_sem=x_recv.at[0],
            device_id=(z, (ex + 1) % NE), device_id_type=MESH,
        ).wait_send()

    def arrive(dst, recv, own, g):
        @pl.when(g == 0)
        def _():
            loads[own].wait()
            wait_recv(dst.at[pl.ds(1, GROUP - 1)], recv.at[0])

        @pl.when(g > 0)
        def _():
            wait_recv(dst.at[pl.ds(GROUP * g, GROUP)], recv.at[g])

    def over_z(src, dst, send, recv, j):
        return pltpu.make_async_remote_copy(
            src_ref=src, dst_ref=dst, send_sem=send, recv_sem=recv,
            device_id=((z + j) % NZ, ex), device_id_type=MESH,
        )

    def give_back(slot):
        if slot == 0:
            return [
                pltpu.make_async_copy(pg.at[0], back.at[ex], loc_sem.at[2]),
                pltpu.make_async_copy(pc.at[0], back_c.at[ex], loc_sem.at[3]),
            ]
        if slot == 1:
            to = ex + 1 - 2 * c
        else:
            i, core = (slot - 2) // 2, slot % 2
            dx, dy = offset(i, core)
            to = expert_at(x - dx, y - dy, core)
        return [
            pltpu.make_async_remote_copy(
                src_ref=src.at[slot], dst_ref=dst.at[ex], send_sem=send, recv_sem=recv,
                device_id=(z, to), device_id_type=MESH,
            )
            for src, dst, send, recv in ((pg, back, pg_send, pg_recv), (pc, back_c, pc_send, pc_recv))
        ]

    for load in loads[:3]:
        load.wait()

    KC = 1024

    def group_step(g, carry):
        base = pl.multiple_of(GROUP * g, GROUP)
        rows = pl.ds(pl.multiple_of(g * ROWS, ROWS), ROWS)
        arrive(xr, x_recv, 3, g)
        for j in (2, 1, 3):
            cols = pl.ds(pl.multiple_of((z + j) % NZ * SLICE, SLICE), SLICE)
            over_z(xr.at[pl.ds(base, GROUP), :, cols], xz.at[j - 1, pl.ds(base, GROUP)], xz_send, xz_recv, j).start()

        fa[...] = jnp.zeros_like(fa)
        fb[...] = jnp.zeros_like(fb)

        def forward(k, cc):
            kk = pl.ds(pl.multiple_of(k * KC, KC), KC)
            xk = xr[pl.ds(base, GROUP), :, kk].reshape(ROWS, KC)
            fa[...] += jnp.dot(xk, wg[kk, :], preferred_element_type=jnp.float32)
            fb[...] += jnp.dot(xk, wu[kk, :], preferred_element_type=jnp.float32)
            return cc

        lax.fori_loop(0, D // KC, forward, 0)
        gate = fa[...]
        upper = fb[...]
        sigma = 1.0 / (1.0 + jnp.exp(-gate))
        swish = gate * sigma
        hidden = (swish * upper).astype(jnp.bfloat16)
        hid[rows, :] = hidden
        fa[...] = upper * sigma * (1.0 + gate * (1.0 - sigma))
        fb[...] = swish

        arrive(dyr, dy_recv, 4, g)

        @pl.when(g == GROUPS - 1)
        def _():
            for slot in range(NE - GROUP):
                for copy in give_back(slot):
                    copy.start()

        def backward(k, hg):
            kk = pl.ds(pl.multiple_of(k * KC, KC), KC)
            dk = dyr[pl.ds(base, GROUP), :, kk].reshape(ROWS, KC)
            return hg + nt(dk, wd[:, kk])

        hg = lax.fori_loop(0, D // KC, backward, jnp.zeros((ROWS, HID), jnp.float32))
        gown[rows, pl.ds(0, HID)] = (hg * fa[...]).astype(jnp.bfloat16)
        gown[rows, pl.ds(HID, HID)] = (hg * fb[...]).astype(jnp.bfloat16)
        for j in (2, 1, 3):
            over_z(gown.at[rows], gz.at[j - 1, rows], gz_send, gz_recv, j).start()
        total = jnp.sum(hid[rows, :].astype(jnp.float32) * hg, axis=1, keepdims=True)
        total = jnp.broadcast_to(total, (ROWS, 128))
        high = total.astype(jnp.bfloat16).astype(jnp.float32)
        lane = lax.broadcasted_iota(jnp.int32, (ROWS, 128), 1)
        pc[pl.ds(base, GROUP)] = (
            jnp.where(lane < 64, high, total - high).astype(jnp.bfloat16).reshape(GROUP, CAP, 128)
        )

        def inward(k, cc):
            kk = pl.ds(pl.multiple_of(k * KC, KC), KC)
            part = nt(gown[rows, pl.ds(0, HID)], wg[kk, :]) + nt(gown[rows, pl.ds(HID, HID)], wu[kk, :])
            pg[pl.ds(base, GROUP), :, kk] = part.astype(jnp.bfloat16).reshape(GROUP, CAP, KC)
            return cc

        lax.fori_loop(0, D // KC, inward, 0)
        return carry

    lax.fori_loop(0, GROUPS, group_step, 0)
    for slot in range(NE - GROUP, NE):
        for copy in give_back(slot):
            copy.start()

    def down_part(j):
        cols = pl.ds(pl.multiple_of((z + j) % NZ * SLICE, SLICE), SLICE)
        total = jnp.zeros((HID, SLICE), jnp.float32)

        def add(g, total):
            rows = pl.ds(pl.multiple_of(g * ROWS, ROWS), ROWS)
            dk = dyr[pl.ds(pl.multiple_of(GROUP * g, GROUP), GROUP), :, cols].reshape(ROWS, SLICE)
            return total + tn(hid[rows, :], dk)

        return lax.fori_loop(0, GROUPS, add, total)

    for j in (2, 1, 3):
        dn_out[j - 1] = down_part(j).astype(jnp.bfloat16)
        over_z(dn_out.at[j - 1], dn_in.at[j - 1], dn_send, dn_recv, j).start()

    wait_recv(xz, xz_recv)
    wait_recv(gz, gz_recv)
    CB = 256

    def wide(k, carry):
        off = pl.multiple_of(k * CB, CB)
        mine = pl.ds(pl.multiple_of(z * SLICE + off, CB), CB)
        total = tn(xr[:, :, mine].reshape(NE * CAP, CB), gown[...])
        for j in range(NZ - 1):
            total += tn(xz[j, :, :, pl.ds(off, CB)].reshape(NE * CAP, CB), gz[j])
        out_g[pl.ds(off, CB), :] = total[:, :HID].astype(jnp.bfloat16)
        out_u[pl.ds(off, CB), :] = total[:, HID:].astype(jnp.bfloat16)
        return carry

    lax.fori_loop(0, SLICE // CB, wide, 0)

    wait_recv(dn_in, dn_recv)
    own = down_part(0)
    for j in range(NZ - 1):
        own += dn_in[j].astype(jnp.float32)
    out_d[...] = own.astype(jnp.bfloat16)

    most = pl.ds(0, NE - 1)
    wait_send(sx.at[most], x_send)
    wait_send(sdy.at[most], dy_send)
    wait_send(xz, xz_send)
    wait_send(gz, gz_send)
    wait_send(dn_out, dn_send)
    wait_send(pg.at[most], pg_send)
    wait_send(pc.at[most], pc_send)
    for copy in give_back(0):
        copy.wait()
    wait_recv(back.at[most], pg_recv)
    wait_recv(back_c.at[most], pc_recv)


def exchange(send_x, send_dy, w_gate, w_up, w_down):
    bf = jnp.bfloat16
    any_ = pl.BlockSpec(memory_space=pl.ANY)
    vm = pl.BlockSpec(memory_space=pltpu.VMEM)
    dma = pltpu.SemaphoreType.DMA
    return pl.pallas_call(
        kernel,
        out_shape=(
            jax.ShapeDtypeStruct((NE, CAP, D), bf),
            jax.ShapeDtypeStruct((NE, CAP, 128), bf),
            jax.ShapeDtypeStruct((SLICE, HID), bf),
            jax.ShapeDtypeStruct((SLICE, HID), bf),
            jax.ShapeDtypeStruct((HID, SLICE), bf),
        ),
        in_specs=[any_] * 5,
        out_specs=(any_, any_, vm, vm, vm),
        scratch_shapes=[
            pltpu.VMEM((NE, CAP, D), bf),
            pltpu.VMEM((NE, CAP, D), bf),
            pltpu.VMEM((NE, CAP, D), bf),
            pltpu.VMEM((NE, CAP, 128), bf),
            pltpu.VMEM((D, HID), bf),
            pltpu.VMEM((D, HID), bf),
            pltpu.VMEM((HID, D), bf),
            pltpu.VMEM((NZ - 1, NE, CAP, SLICE), bf),
            pltpu.VMEM((NZ - 1, NE * CAP, 2 * HID), bf),
            pltpu.VMEM((NE * CAP, 2 * HID), bf),
            pltpu.VMEM((NE * CAP, HID), bf),
            pltpu.VMEM((NZ - 1, HID, SLICE), bf),
            pltpu.VMEM((NZ - 1, HID, SLICE), bf),
            pltpu.VMEM((ROWS, HID), jnp.float32),
            pltpu.VMEM((ROWS, HID), jnp.float32),
            dma((3,)), dma((4,)), dma((GROUPS,)), dma((GROUPS,)),
        ] + [dma] * 12,
        compiler_params=pltpu.CompilerParams(
            collective_id=0, has_side_effects=True, vmem_limit_bytes=63 * 2**20
        ),
    )(send_x, send_dy, w_gate, w_up, w_down)


def on_device(tokens, grad_out, expert_ids, combine, w_gate, w_up, w_down):
    bf = jnp.bfloat16
    rows = tokens.shape[0]
    labels = jnp.arange(NE, dtype=jnp.int32)
    hits = [(expert_ids[:, k, None] == labels[None, :]).astype(bf) for k in range(2)]
    order = jnp.arange(rows, dtype=jnp.int32)
    before = (order[None, :] < order[:, None]).astype(bf)
    earlier = jnp.dot(before, hits[0] + hits[1], preferred_element_type=jnp.float32)
    places = [
        expert_ids[:, k] * CAP + jnp.sum(earlier * hits[k].astype(jnp.float32), axis=1).astype(jnp.int32)
        for k in range(2)
    ]
    slots = jnp.arange(NE * CAP, dtype=jnp.int32)
    put = [(slots[:, None] == places[k][None, :]).astype(bf) for k in range(2)]
    put_x = put[0] + put[1]
    put_dy = put[0] * combine[:, 0][None, :] + put[1] * combine[:, 1][None, :]
    send_x = jnp.dot(put_x, tokens, preferred_element_type=jnp.float32).astype(bf)
    send_dy = jnp.dot(put_dy, grad_out, preferred_element_type=jnp.float32).astype(bf)
    back, back_c, grad_gate, grad_up, grad_down = exchange(
        send_x.reshape(NE, CAP, D), send_dy.reshape(NE, CAP, D), w_gate[0], w_up[0], w_down[0]
    )
    grad_tokens = lax.dot_general(
        put_x, back.reshape(NE * CAP, D), (((0,), (0,)), ((), ())), preferred_element_type=jnp.float32
    ).astype(bf)
    sums = back_c.reshape(NE * CAP, 128)
    parts = [
        lax.dot_general(put[k], sums, (((0,), (0,)), ((), ())), preferred_element_type=jnp.float32)
        for k in range(2)
    ]
    grad_combine = jnp.stack([p[:, 0] + p[:, 64] for p in parts], axis=1) / combine.astype(jnp.float32)
    return grad_tokens, grad_combine.astype(bf), grad_gate[None], grad_up[None], grad_down[None]


def solution(mesh):
    return jax.shard_map(
        on_device,
        mesh=mesh,
        in_specs=(
            P(("dp", "expert"), None),
            P(("dp", "expert"), None),
            P(("dp", "expert"), None),
            P(("dp", "expert"), None),
            P("expert", None, None),
            P("expert", None, None),
            P("expert", None, None),
        ),
        out_specs=(
            P(("dp", "expert"), None),
            P(("dp", "expert"), None),
            P("expert", "dp", None),
            P("expert", "dp", None),
            P("expert", None, "dp"),
        ),
        check_vma=False,
    )
```

```python
import jax
import jax.numpy as jnp
from jax import lax
from jax.experimental import pallas as pl
from jax.experimental.pallas import tpu as pltpu
from jax.sharding import PartitionSpec as P

MESH = pl.DeviceIdType.MESH
NX, NY, NZ, NE = 4, 4, 4, 32
CAP = 24
D, HID = 4096, 512
SLICE = D // NZ
GROUP = 8
GROUPS = NE // GROUP
ROWS = GROUP * CAP
TOK = 256
SC = 512
VMEM_BYTES = 63 * 2**20
RETURNS = {2: range(0, 8), 3: range(8, 24)}
OFFSETS = (
    (1, 0), (3, 0), (0, 1), (0, 3), (1, 1), (3, 3), (1, 3), (3, 1),
    (2, 0), (0, 2), (1, 2), (3, 2), (2, 1), (2, 3), (2, 2),
)


def offset(i, core):
    dx, dy = OFFSETS[i]
    return dx + core * (dy - dx), dy + core * (dx - dy)


def expert_at(x, y, core):
    return (y % NY) * (2 * NX) + (x % NX) * 2 + core


def nt(left, right):
    return lax.dot_general(left, right, (((1,), (1,)), ((), ())), preferred_element_type=jnp.float32)


def tn(left, right):
    return lax.dot_general(left, right, (((0,), (0,)), ((), ())), preferred_element_type=jnp.float32)


def kernel(
    ids_t, weight_t, tok_h, dy_h, wg_h, wu_h, wd_h,
    back, sx, sdy, put_t, out_c, wide_h, down_h,
    tokdy, stage, out_gu, out_d, put, put0, put1, put_dy, back_c, xr, dyr, pg, pc, wg, wu, wd, xz, gz, gown, hid, dn_in, dn_rel, fa, fb,
    in_sem, out_sem, st_sem, w_sem, loc_sem, x_recv, dy_recv, x_send, dy_send, pg_recv, pg_send, pc_recv, pc_send,
    xz_recv, xz_send, gz_next, gz_prev, gz_far, gz_send, dn_recv, rel_recv, dn_send,
):
    bf, f32 = jnp.bfloat16, jnp.float32
    z = lax.axis_index("dp")
    ex = lax.axis_index("expert")
    c = ex % 2
    x = (ex // 2) % NX
    y = ex // (2 * NX)

    loads = [
        pltpu.make_async_copy(wg_h, wg, w_sem.at[0]),
        pltpu.make_async_copy(wu_h, wu, w_sem.at[1]),
        pltpu.make_async_copy(wd_h, wd, w_sem.at[2]),
        pltpu.make_async_copy(sx.at[ex], xr.at[0], loc_sem.at[0]),
        pltpu.make_async_copy(sdy.at[ex], dyr.at[0], loc_sem.at[1]),
    ]

    barrier = pltpu.get_barrier_semaphore()

    def greet(k, carry):
        pl.semaphore_signal(barrier, inc=1, device_id=(z, (ex + k) % NE), device_id_type=MESH)
        return carry

    lax.fori_loop(1, NE, greet, 0)
    for j in range(1, NZ):
        pl.semaphore_signal(barrier, inc=1, device_id=((z + j) % NZ, ex), device_id_type=MESH)
    fetch = [pltpu.make_async_copy(tok_h, tokdy.at[0], in_sem.at[0]), pltpu.make_async_copy(dy_h, tokdy.at[1], in_sem.at[1])]
    for load in fetch + loads[:3]:
        load.start()

    ids = [ids_t[k : k + 1, :].astype(f32) for k in range(2)]
    weight = weight_t[...].astype(f32)
    label = lax.broadcasted_iota(jnp.int32, (NE, TOK), 0).astype(f32)
    hits = [(label == ids[k]).astype(f32) for k in range(2)]
    first = lax.broadcasted_iota(jnp.int32, (TOK, TOK), 0)
    second = lax.broadcasted_iota(jnp.int32, (TOK, TOK), 1)
    before = (first < second).astype(f32).astype(bf)
    earlier = jnp.dot((hits[0] + hits[1]).astype(bf), before, preferred_element_type=f32)
    places = [ids[k] * CAP + jnp.sum(earlier * hits[k], axis=0, keepdims=True) for k in range(2)]
    index = lax.broadcasted_iota(jnp.int32, (NE * CAP, TOK), 0).astype(f32)
    put_k = [(index == places[k]).astype(f32) for k in range(2)]
    put[...] = (put_k[0] + put_k[1]).astype(bf)
    put0[...] = put_k[0].astype(bf)
    put1[...] = put_k[1].astype(bf)
    put_dy[...] = (put_k[0] * weight[0:1] + put_k[1] * weight[1:2]).astype(bf)

    def lay_out(which, rows, dst):
        def block(k, carry):
            kk = pl.ds(pl.multiple_of(k * SC, SC), SC)
            half = k % 2
            move = pltpu.make_async_copy(stage.at[half], dst.at[:, :, kk], st_sem.at[half])

            @pl.when(k >= 2)
            def _():
                move.wait()

            made = jnp.dot(rows[...], tokdy[which, :, kk], preferred_element_type=f32)
            stage[half] = made.astype(bf).reshape(NE, CAP, SC)
            move.start()
            return carry

        fetch[which].wait()
        lax.fori_loop(0, D // SC, block, 0)
        for half in range(2):
            pltpu.make_async_copy(stage.at[half], dst.at[:, :, pl.ds(0, SC)], st_sem.at[half]).wait()
        loads[3 + which].start()

    def to_expert(src, dst, send, recv, i, core):
        if i < 0:
            to, slot = ex + 1 - 2 * c, 1
            group = 0
        else:
            dx, dy = offset(i, c)
            to, slot = expert_at(x + dx, y + dy, core), 2 + 2 * i + c
            group = (2 + 2 * i) // GROUP
        return pltpu.make_async_remote_copy(
            src_ref=src.at[to], dst_ref=dst.at[slot], send_sem=send, recv_sem=recv.at[group],
            device_id=(z, to), device_id_type=MESH,
        )

    lay_out(0, put, sx)
    pl.semaphore_wait(barrier, NE - 1 + NZ - 1)
    for g in range(GROUPS):
        for src, dst, send, recv in ((sx, xr, x_send, x_recv), (sdy, dyr, dy_send, dy_recv)):
            if g == 0 and src is sdy:
                lay_out(1, put_dy, sdy)
            for slot in range(GROUP * g, GROUP * (g + 1), 2):
                if slot == 0:
                    to_expert(src, dst, send, recv, -1, 0).start()
                else:
                    for core in range(2):
                        to_expert(src, dst, send, recv, (slot - 2) // 2, core).start()

    def wait_recv(dst, sem):
        pltpu.make_async_remote_copy(
            src_ref=dst, dst_ref=dst, send_sem=x_send, recv_sem=sem,
            device_id=(z, (ex + 1) % NE), device_id_type=MESH,
        ).wait_recv()

    def wait_send(src, sem):
        pltpu.make_async_remote_copy(
            src_ref=src, dst_ref=src, send_sem=sem, recv_sem=x_recv.at[0],
            device_id=(z, (ex + 1) % NE), device_id_type=MESH,
        ).wait_send()

    def arrive(dst, recv, own, g):
        @pl.when(g == 0)
        def _():
            loads[own].wait()
            wait_recv(dst.at[pl.ds(1, GROUP - 1)], recv.at[0])

        @pl.when(g > 0)
        def _():
            wait_recv(dst.at[pl.ds(GROUP * g, GROUP)], recv.at[g])

    def over_z(src, dst, send, recv, j):
        return pltpu.make_async_remote_copy(
            src_ref=src, dst_ref=dst, send_sem=send, recv_sem=recv,
            device_id=((z + j) % NZ, ex), device_id_type=MESH,
        )

    def give_back(slot):
        if slot == 0:
            return [
                pltpu.make_async_copy(pg.at[0], back.at[ex], loc_sem.at[2]),
                pltpu.make_async_copy(pc.at[0], back_c.at[ex], loc_sem.at[3]),
            ]
        if slot == 1:
            to = ex + 1 - 2 * c
        else:
            i, core = (slot - 2) // 2, slot % 2
            dx, dy = offset(i, core)
            to = expert_at(x - dx, y - dy, core)
        return [
            pltpu.make_async_remote_copy(
                src_ref=src.at[slot], dst_ref=dst.at[ex], send_sem=send, recv_sem=recv,
                device_id=(z, to), device_id_type=MESH,
            )
            for src, dst, send, recv in ((pg, back, pg_send, pg_recv), (pc, back_c, pc_send, pc_recv))
        ]

    for k in range(NE * CAP // TOK):
        part = pl.ds(k * TOK, TOK)
        put_t[:, part] = put[part, :].astype(f32).T.astype(bf)

    for load in loads[:3]:
        load.wait()

    def pass_on(g):
        rows = pl.ds(pl.multiple_of(g * ROWS, ROWS), ROWS)
        wait_recv(gz.at[0, rows], gz_next.at[g])
        low = pl.ds(pl.multiple_of(g * ROWS, ROWS // 2), ROWS // 2)
        over_z(gz.at[0, low], gz.at[1, low], gz_send, gz_far, 1).start()
        wait_recv(gz.at[2, rows], gz_prev.at[g])
        high = pl.ds(pl.multiple_of(g * ROWS + ROWS // 2, ROWS // 2), ROWS // 2)
        over_z(gz.at[2, high], gz.at[1, high], gz_send, gz_far, 3).start()

    KC = 1024

    def group_step(g, carry):
        base = pl.multiple_of(GROUP * g, GROUP)
        rows = pl.ds(pl.multiple_of(g * ROWS, ROWS), ROWS)
        arrive(xr, x_recv, 3, g)
        for j in (2, 1, 3):
            cols = pl.ds(pl.multiple_of((z + j) % NZ * SLICE, SLICE), SLICE)
            over_z(xr.at[pl.ds(base, GROUP), :, cols], xz.at[j - 1, pl.ds(base, GROUP)], xz_send, xz_recv, j).start()

        fa[...] = jnp.zeros_like(fa)
        fb[...] = jnp.zeros_like(fb)

        def forward(k, cc):
            kk = pl.ds(pl.multiple_of(k * KC, KC), KC)
            xk = xr[pl.ds(base, GROUP), :, kk].reshape(ROWS, KC)
            fa[...] += jnp.dot(xk, wg[kk, :], preferred_element_type=jnp.float32)
            fb[...] += jnp.dot(xk, wu[kk, :], preferred_element_type=jnp.float32)
            return cc

        lax.fori_loop(0, D // KC, forward, 0)
        gate = fa[...]
        upper = fb[...]
        sigma = 1.0 / (1.0 + jnp.exp(-gate))
        swish = gate * sigma
        hidden = (swish * upper).astype(jnp.bfloat16)
        hid[rows, :] = hidden
        fa[...] = upper * sigma * (1.0 + gate * (1.0 - sigma))
        fb[...] = swish

        @pl.when(g >= 1)
        def _():
            pass_on(g - 1)

        arrive(dyr, dy_recv, 4, g)

        for step, slots in RETURNS.items():

            @pl.when(g == step)
            def _():
                for slot in slots:
                    for copy in give_back(slot):
                        copy.start()

        def backward(k, hg):
            kk = pl.ds(pl.multiple_of(k * KC, KC), KC)
            dk = dyr[pl.ds(base, GROUP), :, kk].reshape(ROWS, KC)
            return hg + nt(dk, wd[:, kk])

        hg = lax.fori_loop(0, D // KC, backward, jnp.zeros((ROWS, HID), jnp.float32))
        gown[rows, pl.ds(0, HID)] = (hg * fa[...]).astype(jnp.bfloat16)
        gown[rows, pl.ds(HID, HID)] = (hg * fb[...]).astype(jnp.bfloat16)
        over_z(gown.at[rows], gz.at[0, rows], gz_send, gz_next.at[g], 1).start()
        over_z(gown.at[rows], gz.at[2, rows], gz_send, gz_prev.at[g], 3).start()
        total = jnp.sum(hid[rows, :].astype(jnp.float32) * hg, axis=1, keepdims=True)
        total = jnp.broadcast_to(total, (ROWS, 128))
        high = total.astype(jnp.bfloat16).astype(jnp.float32)
        lane = lax.broadcasted_iota(jnp.int32, (ROWS, 128), 1)
        pc[pl.ds(base, GROUP)] = (
            jnp.where(lane < 64, high, total - high).astype(jnp.bfloat16).reshape(GROUP, CAP, 128)
        )

        def inward(k, cc):
            kk = pl.ds(pl.multiple_of(k * KC, KC), KC)
            part = nt(gown[rows, pl.ds(0, HID)], wg[kk, :]) + nt(gown[rows, pl.ds(HID, HID)], wu[kk, :])
            pg[pl.ds(base, GROUP), :, kk] = part.astype(jnp.bfloat16).reshape(GROUP, CAP, KC)
            return cc

        lax.fori_loop(0, D // KC, inward, 0)
        return carry

    lax.fori_loop(0, GROUPS, group_step, 0)
    for slot in range(NE - GROUP, NE):
        for copy in give_back(slot):
            copy.start()

    pass_on(GROUPS - 1)

    def down_part(j):
        cols = pl.ds(pl.multiple_of((z + j) % NZ * SLICE, SLICE), SLICE)
        total = jnp.zeros((HID, SLICE), jnp.float32)

        def add(g, total):
            rows = pl.ds(pl.multiple_of(g * ROWS, ROWS), ROWS)
            dk = dyr[pl.ds(pl.multiple_of(GROUP * g, GROUP), GROUP), :, cols].reshape(ROWS, SLICE)
            return total + tn(hid[rows, :], dk)

        return lax.fori_loop(0, GROUPS, add, total)

    half = HID // 2
    low, high = pl.ds(0, half), pl.ds(half, half)

    def dn_out(h, j):
        return tokdy.at[h, :, pl.ds((j - 1) * SLICE, SLICE)]

    def make_down(j):
        part = down_part(j).astype(bf)
        dn_out(0, j)[...] = part[:half]
        dn_out(1, j)[...] = part[half:]

    make_down(2)
    over_z(dn_out(0, 2), dn_rel.at[0], dn_send, rel_recv.at[0], 1).start()
    over_z(dn_out(1, 2), dn_rel.at[1], dn_send, rel_recv.at[1], 3).start()
    make_down(1)
    over_z(dn_out(1, 1), dn_in.at[0, high], dn_send, dn_recv, 1).start()
    make_down(3)
    over_z(dn_out(0, 3), dn_in.at[1, low], dn_send, dn_recv, 3).start()

    wait_recv(xz, xz_recv)
    wait_recv(gz.at[1], gz_far)
    CB = 256

    def wide(k, carry):
        off = pl.multiple_of(k * CB, CB)
        mine = pl.ds(pl.multiple_of(z * SLICE + off, CB), CB)
        total = tn(xr[:, :, mine].reshape(NE * CAP, CB), gown[...])
        for j in range(NZ - 1):
            total += tn(xz[j, :, :, pl.ds(off, CB)].reshape(NE * CAP, CB), gz[j])
        out_gu[pl.ds(off, CB), :] = total.astype(bf)
        return carry

    lax.fori_loop(0, SLICE // CB, wide, 0)
    wide_out = pltpu.make_async_copy(out_gu, wide_h, out_sem.at[0])
    wide_out.start()

    for h, j in ((0, 1), (1, 3)):
        wait_recv(dn_rel.at[h], rel_recv.at[h])
        dn_out(h, j)[...] = (dn_out(h, j)[...].astype(f32) + dn_rel[h].astype(f32)).astype(bf)
        over_z(dn_out(h, j), dn_in.at[h, high if h else low], dn_send, dn_recv, j).start()
    own = down_part(0)
    wait_recv(dn_in, dn_recv)
    for j in range(2):
        own += dn_in[j].astype(f32)
    out_d[...] = own.astype(bf)
    down_out = pltpu.make_async_copy(out_d, down_h, out_sem.at[1])
    down_out.start()

    most = pl.ds(0, NE - 1)
    wait_send(sx.at[most], x_send)
    wait_send(sdy.at[most], dy_send)
    wait_send(xz, xz_send)
    wait_send(gz, gz_send)
    wait_send(tokdy.at[:, :, pl.ds(0, (NZ - 1) * SLICE)], dn_send)
    wait_send(pg.at[most], pg_send)
    wait_send(pc.at[most], pc_send)
    for copy in give_back(0):
        copy.wait()
    wait_recv(back_c.at[most], pc_recv)
    sums = back_c[...].reshape(NE * CAP, 128)
    both = [tn(rows[...], sums) for rows in (put0, put1)]
    lane = lax.broadcasted_iota(jnp.int32, (TOK, 128), 1)
    out_c[...] = jnp.where(
        lane == 0,
        jnp.sum(jnp.where(lane % 64 == 0, both[0], 0.0), axis=1, keepdims=True),
        jnp.sum(jnp.where(lane % 64 == 0, both[1], 0.0), axis=1, keepdims=True),
    )
    wait_recv(back.at[most], pg_recv)
    wide_out.wait()
    down_out.wait()


def exchange(ids_t, weight_t, tokens, grad_out, w_gate, w_up, w_down):
    bf, f32 = jnp.bfloat16, jnp.float32
    any_ = pl.BlockSpec(memory_space=pl.ANY)
    vm = pl.BlockSpec(memory_space=pltpu.VMEM)
    dma = pltpu.SemaphoreType.DMA
    return pl.pallas_call(
        kernel,
        out_shape=(
            jax.ShapeDtypeStruct((NE, CAP, D), bf),
            jax.ShapeDtypeStruct((NE, CAP, D), bf),
            jax.ShapeDtypeStruct((NE, CAP, D), bf),
            jax.ShapeDtypeStruct((TOK, NE * CAP), bf),
            jax.ShapeDtypeStruct((TOK, 128), f32),
            jax.ShapeDtypeStruct((SLICE, 2 * HID), bf),
            jax.ShapeDtypeStruct((HID, SLICE), bf),
        ),
        in_specs=[vm] * 2 + [any_] * 5,
        out_specs=(any_, any_, any_, vm, vm, any_, any_),
        scratch_shapes=[
            pltpu.VMEM((2, TOK, D), bf),
            pltpu.VMEM((2, NE, CAP, SC), bf),
            pltpu.VMEM((SLICE, 2 * HID), bf),
            pltpu.VMEM((HID, SLICE), bf),
            pltpu.VMEM((NE * CAP, TOK), bf),
            pltpu.VMEM((NE * CAP, TOK), bf),
            pltpu.VMEM((NE * CAP, TOK), bf),
            pltpu.VMEM((NE * CAP, TOK), bf),
            pltpu.VMEM((NE, CAP, 128), bf),
            pltpu.VMEM((NE, CAP, D), bf),
            pltpu.VMEM((NE, CAP, D), bf),
            pltpu.VMEM((NE, CAP, D), bf),
            pltpu.VMEM((NE, CAP, 128), bf),
            pltpu.VMEM((D, HID), bf),
            pltpu.VMEM((D, HID), bf),
            pltpu.VMEM((HID, D), bf),
            pltpu.VMEM((NZ - 1, NE, CAP, SLICE), bf),
            pltpu.VMEM((NZ - 1, NE * CAP, 2 * HID), bf),
            pltpu.VMEM((NE * CAP, 2 * HID), bf),
            pltpu.VMEM((NE * CAP, HID), bf),
            pltpu.VMEM((2, HID, SLICE), bf),
            pltpu.VMEM((2, HID // 2, SLICE), bf),
            pltpu.VMEM((ROWS, HID), f32),
            pltpu.VMEM((ROWS, HID), f32),
            dma((2,)), dma((2,)), dma((2,)), dma((3,)), dma((4,)), dma((GROUPS,)), dma((GROUPS,)),
        ] + [dma] * 6 + [dma] * 2 + [dma((GROUPS,)), dma((GROUPS,)), dma, dma, dma, dma((2,)), dma],
        compiler_params=pltpu.CompilerParams(
            collective_id=0, has_side_effects=True, vmem_limit_bytes=VMEM_BYTES
        ),
    )(ids_t, weight_t, tokens, grad_out, w_gate, w_up, w_down)


def finish_kernel(put_t, back, wide, down, grad_tokens, grad_gate, grad_up, grad_down):
    grad_tokens[...] = jnp.dot(put_t[...], back[...], preferred_element_type=jnp.float32).astype(jnp.bfloat16)
    grad_gate[...] = wide[:, :HID]
    grad_up[...] = wide[:, HID:]
    grad_down[...] = down[...]


def finish(put_t, back, wide, down):
    bf = jnp.bfloat16
    steps = 8
    return pl.pallas_call(
        finish_kernel,
        grid=(steps,),
        out_shape=(
            jax.ShapeDtypeStruct((TOK, D), bf),
            jax.ShapeDtypeStruct((SLICE, HID), bf),
            jax.ShapeDtypeStruct((SLICE, HID), bf),
            jax.ShapeDtypeStruct((HID, SLICE), bf),
        ),
        in_specs=[
            pl.BlockSpec((TOK, NE * CAP), lambda k: (0, 0)),
            pl.BlockSpec((NE * CAP, D // steps), lambda k: (0, k)),
            pl.BlockSpec((SLICE // steps, 2 * HID), lambda k: (k, 0)),
            pl.BlockSpec((HID // steps, SLICE), lambda k: (k, 0)),
        ],
        out_specs=(
            pl.BlockSpec((TOK, D // steps), lambda k: (0, k)),
            pl.BlockSpec((SLICE // steps, HID), lambda k: (k, 0)),
            pl.BlockSpec((SLICE // steps, HID), lambda k: (k, 0)),
            pl.BlockSpec((HID // steps, SLICE), lambda k: (k, 0)),
        ),
        compiler_params=pltpu.CompilerParams(vmem_limit_bytes=60 * 2**20),
    )(put_t, back, wide, down)


def on_device(tokens, grad_out, expert_ids, combine, w_gate, w_up, w_down):
    back, _, _, put_t, sums, wide, down = exchange(
        expert_ids.T, combine.T, tokens, grad_out, w_gate[0], w_up[0], w_down[0]
    )
    grad_tokens, grad_gate, grad_up, grad_down = finish(put_t, back.reshape(NE * CAP, D), wide, down)
    grad_combine = (sums[:, :2] / combine.astype(jnp.float32)).astype(jnp.bfloat16)
    return grad_tokens, grad_combine, grad_gate[None], grad_up[None], grad_down[None]


def solution(mesh):
    return jax.shard_map(
        on_device,
        mesh=mesh,
        in_specs=(
            P(("dp", "expert"), None),
            P(("dp", "expert"), None),
            P(("dp", "expert"), None),
            P(("dp", "expert"), None),
            P("expert", None, None),
            P("expert", None, None),
            P("expert", None, None),
        ),
        out_specs=(
            P(("dp", "expert"), None),
            P(("dp", "expert"), None),
            P("expert", "dp", None),
            P("expert", "dp", None),
            P("expert", None, "dp"),
        ),
        check_vma=False,
    )
```

```python
import jax
import jax.numpy as jnp
from jax import lax
from jax.experimental import pallas as pl
from jax.experimental.pallas import tpu as pltpu
from jax.sharding import PartitionSpec as P

MESH = pl.DeviceIdType.MESH
NX, NY, NZ, NE = 4, 4, 4, 32
CAP = 24
D, HID = 4096, 512
SLICE = D // NZ
GROUP = 8
GROUPS = NE // GROUP
ROWS = GROUP * CAP
TOK = 256
PARTNER, OWN = NE - 2, NE - 1
SC = 2048
VMEM_BYTES = 63 * 2**20
RETURNS = {2: range(0, 8), 3: range(8, 24)}
OFFSETS = (
    (1, 0), (3, 0), (0, 1), (0, 3), (1, 1), (3, 3), (1, 3), (3, 1),
    (2, 0), (0, 2), (1, 2), (3, 2), (2, 1), (2, 3), (2, 2),
)


def offset(i, core):
    dx, dy = OFFSETS[i]
    return dx + core * (dy - dx), dy + core * (dx - dy)


def expert_at(x, y, core):
    return (y % NY) * (2 * NX) + (x % NX) * 2 + core


def nt(left, right):
    return lax.dot_general(left, right, (((1,), (1,)), ((), ())), preferred_element_type=jnp.float32)


def tn(left, right):
    return lax.dot_general(left, right, (((0,), (0,)), ((), ())), preferred_element_type=jnp.float32)


def kernel(
    ids_t, weight_t, tok_h, dy_h, wg_h, wu_h, wd_h,
    back, sx, sdy, put_t, out_c, wide_h, down_h,
    tokdy, stage, out_gu, out_d, put, put0, put1, put_dy, back_c, xr, dyr, pg, pc, wg, wu, wd, xz, gz, gown, hid, dn_in, dn_rel, fa, fb,
    in_sem, out_sem, st_sem, w_sem, loc_sem, x_recv, dy_recv, x_send, dy_send, pg_recv, pg_send, pc_recv, pc_send,
    xz_recv, xz_send, gz_next, gz_prev, gz_far, gz_send, dn_recv, rel_recv, dn_send,
):
    bf, f32 = jnp.bfloat16, jnp.float32
    z = lax.axis_index("dp")
    ex = lax.axis_index("expert")
    c = ex % 2
    x = (ex // 2) % NX
    y = ex // (2 * NX)

    loads = [
        pltpu.make_async_copy(wg_h, wg, w_sem.at[0]),
        pltpu.make_async_copy(wu_h, wu, w_sem.at[1]),
        pltpu.make_async_copy(wd_h, wd, w_sem.at[2]),
        pltpu.make_async_copy(sx.at[OWN], xr.at[OWN], loc_sem.at[0]),
        pltpu.make_async_copy(sdy.at[OWN], dyr.at[OWN], loc_sem.at[1]),
    ]

    barrier = pltpu.get_barrier_semaphore()

    def greet(k, carry):
        pl.semaphore_signal(barrier, inc=1, device_id=(z, (ex + k) % NE), device_id_type=MESH)
        return carry

    lax.fori_loop(1, NE, greet, 0)
    for j in range(1, NZ):
        pl.semaphore_signal(barrier, inc=1, device_id=((z + j) % NZ, ex), device_id_type=MESH)
    fetch = [pltpu.make_async_copy(tok_h, tokdy.at[0], in_sem.at[0]), pltpu.make_async_copy(dy_h, tokdy.at[1], in_sem.at[1])]
    for load in fetch + loads[:3]:
        load.start()

    ids = [ids_t[k : k + 1, :].astype(f32) for k in range(2)]
    weight = weight_t[...].astype(f32)
    position = lax.broadcasted_iota(jnp.int32, (NE, TOK), 0)
    label = jnp.where(position == OWN, ex, ex + 1 - 2 * c)
    for n in range(PARTNER):
        dx, dy = offset(n // 2, c)
        label = jnp.where(position == n, expert_at(x + dx, y + dy, n % 2), label)
    label = label.astype(f32)
    position = position.astype(f32)
    hits = [(label == ids[k]).astype(f32) for k in range(2)]
    first = lax.broadcasted_iota(jnp.int32, (TOK, TOK), 0)
    second = lax.broadcasted_iota(jnp.int32, (TOK, TOK), 1)
    before = (first < second).astype(f32).astype(bf)
    earlier = jnp.dot((hits[0] + hits[1]).astype(bf), before, preferred_element_type=f32)
    places = [jnp.sum((position * CAP + earlier) * hits[k], axis=0, keepdims=True) for k in range(2)]
    index = lax.broadcasted_iota(jnp.int32, (NE * CAP, TOK), 0).astype(f32)
    put_k = [(index == places[k]).astype(f32) for k in range(2)]
    put[...] = (put_k[0] + put_k[1]).astype(bf)
    put0[...] = put_k[0].astype(bf)
    put1[...] = put_k[1].astype(bf)
    put_dy[...] = (put_k[0] * weight[0:1] + put_k[1] * weight[1:2]).astype(bf)

    def to_expert(src, dst, send, recv, n):
        if n == PARTNER:
            to, slot = ex + 1 - 2 * c, PARTNER
        else:
            i, core = n // 2, n % 2
            dx, dy = offset(i, c)
            to, slot = expert_at(x + dx, y + dy, core), 2 * i + c
        return pltpu.make_async_remote_copy(
            src_ref=src.at[n], dst_ref=dst.at[slot], send_sem=send, recv_sem=recv.at[n // GROUP],
            device_id=(z, to), device_id_type=MESH,
        )

    kinds = ((put, sx, xr, x_send, x_recv), (put_dy, sdy, dyr, dy_send, dy_recv))

    def stage_out(step, h):
        g, which = divmod(step, 2)
        kk = pl.ds(pl.multiple_of(h * SC, SC), SC)
        return pltpu.make_async_copy(
            stage.at[h], kinds[which][1].at[pl.ds(GROUP * g, GROUP), :, kk], st_sem.at[h]
        )

    def leave(step):
        g, which = divmod(step, 2)
        _, src, dst, send, recv = kinds[which]
        for n in range(GROUP * g, GROUP * (g + 1)):
            if n == OWN:
                loads[3 + which].start()
            else:
                to_expert(src, dst, send, recv, n).start()

    for step in range(2 * GROUPS):
        g, which = divmod(step, 2)
        if g == 0:
            fetch[which].wait()

        def lay_out(h, carry):
            if step > 0:
                stage_out(step - 1, h).wait()
            kk = pl.ds(pl.multiple_of(h * SC, SC), SC)
            made = jnp.dot(kinds[which][0][pl.ds(g * ROWS, ROWS), :], tokdy[which, :, kk], preferred_element_type=f32)
            stage[h] = made.reshape(GROUP, CAP, SC).astype(bf)
            stage_out(step, h).start()
            return carry

        lax.fori_loop(0, D // SC, lay_out, 0)
        if step == 1:
            pl.semaphore_wait(barrier, NE - 1 + NZ - 1)
        if step > 0:
            leave(step - 1)
    for h in range(D // SC):
        stage_out(2 * GROUPS - 1, h).wait()
    leave(2 * GROUPS - 1)

    def wait_recv(dst, sem):
        pltpu.make_async_remote_copy(
            src_ref=dst, dst_ref=dst, send_sem=x_send, recv_sem=sem,
            device_id=(z, (ex + 1) % NE), device_id_type=MESH,
        ).wait_recv()

    def wait_send(src, sem):
        pltpu.make_async_remote_copy(
            src_ref=src, dst_ref=src, send_sem=sem, recv_sem=x_recv.at[0],
            device_id=(z, (ex + 1) % NE), device_id_type=MESH,
        ).wait_send()

    def arrive(dst, recv, own, g):
        @pl.when(g == GROUPS - 1)
        def _():
            loads[own].wait()
            wait_recv(dst.at[pl.ds(NE - GROUP, GROUP - 1)], recv.at[GROUPS - 1])

        @pl.when(g < GROUPS - 1)
        def _():
            wait_recv(dst.at[pl.ds(GROUP * g, GROUP)], recv.at[g])

    def over_z(src, dst, send, recv, j):
        return pltpu.make_async_remote_copy(
            src_ref=src, dst_ref=dst, send_sem=send, recv_sem=recv,
            device_id=((z + j) % NZ, ex), device_id_type=MESH,
        )

    def give_back(slot):
        if slot == OWN:
            return [
                pltpu.make_async_copy(pg.at[OWN], back.at[OWN], loc_sem.at[2]),
                pltpu.make_async_copy(pc.at[OWN], back_c.at[OWN], loc_sem.at[3]),
            ]
        if slot == PARTNER:
            to, n = ex + 1 - 2 * c, PARTNER
        else:
            i, core = slot // 2, slot % 2
            dx, dy = offset(i, core)
            to, n = expert_at(x - dx, y - dy, core), 2 * i + c
        return [
            pltpu.make_async_remote_copy(
                src_ref=src.at[slot], dst_ref=dst.at[n], send_sem=send, recv_sem=recv,
                device_id=(z, to), device_id_type=MESH,
            )
            for src, dst, send, recv in ((pg, back, pg_send, pg_recv), (pc, back_c, pc_send, pc_recv))
        ]

    for k in range(NE * CAP // TOK):
        part = pl.ds(k * TOK, TOK)
        put_t[:, part] = put[part, :].astype(f32).T.astype(bf)

    for load in loads[:3]:
        load.wait()

    def pass_on(g):
        rows = pl.ds(pl.multiple_of(g * ROWS, ROWS), ROWS)
        wait_recv(gz.at[0, rows], gz_next.at[g])
        low = pl.ds(pl.multiple_of(g * ROWS, ROWS // 2), ROWS // 2)
        over_z(gz.at[0, low], gz.at[1, low], gz_send, gz_far, 1).start()
        wait_recv(gz.at[2, rows], gz_prev.at[g])
        high = pl.ds(pl.multiple_of(g * ROWS + ROWS // 2, ROWS // 2), ROWS // 2)
        over_z(gz.at[2, high], gz.at[1, high], gz_send, gz_far, 3).start()

    KC = 1024

    def group_step(g, carry):
        base = pl.multiple_of(GROUP * g, GROUP)
        rows = pl.ds(pl.multiple_of(g * ROWS, ROWS), ROWS)
        arrive(xr, x_recv, 3, g)
        for j in (2, 1, 3):
            cols = pl.ds(pl.multiple_of((z + j) % NZ * SLICE, SLICE), SLICE)
            over_z(xr.at[pl.ds(base, GROUP), :, cols], xz.at[j - 1, pl.ds(base, GROUP)], xz_send, xz_recv, j).start()

        fa[...] = jnp.zeros_like(fa)
        fb[...] = jnp.zeros_like(fb)

        def forward(k, cc):
            kk = pl.ds(pl.multiple_of(k * KC, KC), KC)
            xk = xr[pl.ds(base, GROUP), :, kk].reshape(ROWS, KC)
            fa[...] += jnp.dot(xk, wg[kk, :], preferred_element_type=jnp.float32)
            fb[...] += jnp.dot(xk, wu[kk, :], preferred_element_type=jnp.float32)
            return cc

        lax.fori_loop(0, D // KC, forward, 0)
        gate = fa[...]
        upper = fb[...]
        sigma = 1.0 / (1.0 + jnp.exp(-gate))
        swish = gate * sigma
        hidden = (swish * upper).astype(jnp.bfloat16)
        hid[rows, :] = hidden
        fa[...] = upper * sigma * (1.0 + gate * (1.0 - sigma))
        fb[...] = swish

        @pl.when(g >= 1)
        def _():
            pass_on(g - 1)

        for step, slots in RETURNS.items():

            @pl.when(g == step)
            def _():
                for slot in slots:
                    for copy in give_back(slot):
                        copy.start()

        arrive(dyr, dy_recv, 4, g)

        def backward(k, hg):
            kk = pl.ds(pl.multiple_of(k * KC, KC), KC)
            dk = dyr[pl.ds(base, GROUP), :, kk].reshape(ROWS, KC)
            return hg + nt(dk, wd[:, kk])

        hg = lax.fori_loop(0, D // KC, backward, jnp.zeros((ROWS, HID), jnp.float32))
        gown[rows, pl.ds(0, HID)] = (hg * fa[...]).astype(jnp.bfloat16)
        gown[rows, pl.ds(HID, HID)] = (hg * fb[...]).astype(jnp.bfloat16)
        over_z(gown.at[rows], gz.at[0, rows], gz_send, gz_next.at[g], 1).start()
        over_z(gown.at[rows], gz.at[2, rows], gz_send, gz_prev.at[g], 3).start()
        total = jnp.sum(hid[rows, :].astype(jnp.float32) * hg, axis=1, keepdims=True)
        total = jnp.broadcast_to(total, (ROWS, 128))
        high = total.astype(jnp.bfloat16).astype(jnp.float32)
        lane = lax.broadcasted_iota(jnp.int32, (ROWS, 128), 1)
        pc[pl.ds(base, GROUP)] = (
            jnp.where(lane < 64, high, total - high).reshape(GROUP, CAP, 128).astype(jnp.bfloat16)
        )

        def inward(k, cc):
            kk = pl.ds(pl.multiple_of(k * KC, KC), KC)
            part = nt(gown[rows, pl.ds(0, HID)], wg[kk, :]) + nt(gown[rows, pl.ds(HID, HID)], wu[kk, :])
            pg[pl.ds(base, GROUP), :, kk] = part.reshape(GROUP, CAP, KC).astype(jnp.bfloat16)
            return cc

        lax.fori_loop(0, D // KC, inward, 0)
        return carry

    lax.fori_loop(0, GROUPS, group_step, 0)
    for slot in range(NE - GROUP, NE):
        for copy in give_back(slot):
            copy.start()

    pass_on(GROUPS - 1)

    def down_part(j):
        cols = pl.ds(pl.multiple_of((z + j) % NZ * SLICE, SLICE), SLICE)
        total = jnp.zeros((HID, SLICE), jnp.float32)

        def add(g, total):
            rows = pl.ds(pl.multiple_of(g * ROWS, ROWS), ROWS)
            dk = dyr[pl.ds(pl.multiple_of(GROUP * g, GROUP), GROUP), :, cols].reshape(ROWS, SLICE)
            return total + tn(hid[rows, :], dk)

        return lax.fori_loop(0, GROUPS, add, total)

    half = HID // 2
    low, high = pl.ds(0, half), pl.ds(half, half)

    def dn_out(h, j):
        return tokdy.at[h, :, pl.ds((j - 1) * SLICE, SLICE)]

    def make_down(j):
        part = down_part(j).astype(bf)
        dn_out(0, j)[...] = part[:half]
        dn_out(1, j)[...] = part[half:]

    make_down(2)
    over_z(dn_out(0, 2), dn_rel.at[0], dn_send, rel_recv.at[0], 1).start()
    over_z(dn_out(1, 2), dn_rel.at[1], dn_send, rel_recv.at[1], 3).start()
    make_down(1)
    over_z(dn_out(1, 1), dn_in.at[0, high], dn_send, dn_recv, 1).start()
    make_down(3)
    over_z(dn_out(0, 3), dn_in.at[1, low], dn_send, dn_recv, 3).start()

    wait_recv(xz, xz_recv)
    wait_recv(gz.at[1], gz_far)
    CB = 256

    def wide(k, carry):
        off = pl.multiple_of(k * CB, CB)
        mine = pl.ds(pl.multiple_of(z * SLICE + off, CB), CB)
        total = tn(xr[:, :, mine].reshape(NE * CAP, CB), gown[...])
        for j in range(NZ - 1):
            total += tn(xz[j, :, :, pl.ds(off, CB)].reshape(NE * CAP, CB), gz[j])
        out_gu[pl.ds(off, CB), :] = total.astype(bf)
        return carry

    lax.fori_loop(0, SLICE // CB, wide, 0)
    wide_out = pltpu.make_async_copy(out_gu, wide_h, out_sem.at[0])
    wide_out.start()

    for h, j in ((0, 1), (1, 3)):
        wait_recv(dn_rel.at[h], rel_recv.at[h])
        dn_out(h, j)[...] = (dn_out(h, j)[...].astype(f32) + dn_rel[h].astype(f32)).astype(bf)
        over_z(dn_out(h, j), dn_in.at[h, high if h else low], dn_send, dn_recv, j).start()
    own = down_part(0)
    wait_recv(dn_in, dn_recv)
    for j in range(2):
        own += dn_in[j].astype(f32)
    out_d[...] = own.astype(bf)
    down_out = pltpu.make_async_copy(out_d, down_h, out_sem.at[1])
    down_out.start()

    most = pl.ds(0, NE - 1)
    wait_send(sx.at[most], x_send)
    wait_send(sdy.at[most], dy_send)
    wait_send(xz, xz_send)
    wait_send(gz, gz_send)
    wait_send(tokdy.at[:, :, pl.ds(0, (NZ - 1) * SLICE)], dn_send)
    wait_send(pg.at[most], pg_send)
    wait_send(pc.at[most], pc_send)
    for copy in give_back(OWN):
        copy.wait()
    wait_recv(back_c.at[most], pc_recv)
    sums = back_c[...].reshape(NE * CAP, 128)
    for k, rows in ((0, put0), (1, put1)):
        both = tn(sums, rows[...])
        out_c[k : k + 1, :] = (both[0:1] + both[64:65]) / weight_t[k : k + 1, :].astype(f32)
    wait_recv(back.at[most], pg_recv)
    wide_out.wait()
    down_out.wait()


def exchange(ids_t, weight_t, tokens, grad_out, w_gate, w_up, w_down):
    bf, f32 = jnp.bfloat16, jnp.float32
    any_ = pl.BlockSpec(memory_space=pl.ANY)
    vm = pl.BlockSpec(memory_space=pltpu.VMEM)
    dma = pltpu.SemaphoreType.DMA
    return pl.pallas_call(
        kernel,
        out_shape=(
            jax.ShapeDtypeStruct((NE, CAP, D), bf),
            jax.ShapeDtypeStruct((NE, CAP, D), bf),
            jax.ShapeDtypeStruct((NE, CAP, D), bf),
            jax.ShapeDtypeStruct((TOK, NE * CAP), bf),
            jax.ShapeDtypeStruct((2, TOK), f32),
            jax.ShapeDtypeStruct((SLICE, 2 * HID), bf),
            jax.ShapeDtypeStruct((HID, SLICE), bf),
        ),
        in_specs=[vm] * 2 + [any_] * 5,
        out_specs=(any_, any_, any_, vm, vm, any_, any_),
        scratch_shapes=[
            pltpu.VMEM((2, TOK, D), bf),
            pltpu.VMEM((D // SC, GROUP, CAP, SC), bf),
            pltpu.VMEM((SLICE, 2 * HID), bf),
            pltpu.VMEM((HID, SLICE), bf),
            pltpu.VMEM((NE * CAP, TOK), bf),
            pltpu.VMEM((NE * CAP, TOK), bf),
            pltpu.VMEM((NE * CAP, TOK), bf),
            pltpu.VMEM((NE * CAP, TOK), bf),
            pltpu.VMEM((NE, CAP, 128), bf),
            pltpu.VMEM((NE, CAP, D), bf),
            pltpu.VMEM((NE, CAP, D), bf),
            pltpu.VMEM((NE, CAP, D), bf),
            pltpu.VMEM((NE, CAP, 128), bf),
            pltpu.VMEM((D, HID), bf),
            pltpu.VMEM((D, HID), bf),
            pltpu.VMEM((HID, D), bf),
            pltpu.VMEM((NZ - 1, NE, CAP, SLICE), bf),
            pltpu.VMEM((NZ - 1, NE * CAP, 2 * HID), bf),
            pltpu.VMEM((NE * CAP, 2 * HID), bf),
            pltpu.VMEM((NE * CAP, HID), bf),
            pltpu.VMEM((2, HID, SLICE), bf),
            pltpu.VMEM((2, HID // 2, SLICE), bf),
            pltpu.VMEM((ROWS, HID), f32),
            pltpu.VMEM((ROWS, HID), f32),
            dma((2,)), dma((2,)), dma((2,)), dma((3,)), dma((4,)), dma((GROUPS,)), dma((GROUPS,)),
        ] + [dma] * 6 + [dma] * 2 + [dma((GROUPS,)), dma((GROUPS,)), dma, dma, dma, dma((2,)), dma],
        compiler_params=pltpu.CompilerParams(
            collective_id=0, has_side_effects=True, vmem_limit_bytes=VMEM_BYTES
        ),
    )(ids_t, weight_t, tokens, grad_out, w_gate, w_up, w_down)


def finish_kernel(
    put_t, sums, back, wide, down, grad_tokens, grad_combine, grad_gate, grad_up, grad_down,
    rows, made, wide_v, down_v, load_sem, out_sem,
):
    steps = 4
    width = D // steps
    loads = [
        pltpu.make_async_copy(back.at[:, :, pl.ds(k * width, width)], rows.at[:, :, pl.ds(k * width, width)], load_sem.at[k])
        for k in range(steps)
    ]
    loads.append(pltpu.make_async_copy(wide, wide_v, load_sem.at[steps]))
    loads.append(pltpu.make_async_copy(down, down_v, load_sem.at[steps + 1]))
    for copy in loads:
        copy.start()
    moves = []
    grad_combine[...] = sums[...].astype(jnp.bfloat16)
    for k in range(steps):
        kk = pl.ds(k * width, width)
        loads[k].wait()
        block = rows[:, :, kk].reshape(NE * CAP, width)
        made[:, kk] = jnp.dot(put_t[...], block, preferred_element_type=jnp.float32).astype(jnp.bfloat16)
        moves.append(pltpu.make_async_copy(made.at[:, kk], grad_tokens.at[:, kk], out_sem.at[3 + k]))
        moves[-1].start()
    loads[steps].wait()
    loads[steps + 1].wait()
    for src, dst, sem in (
        (wide_v.at[:, pl.ds(0, HID)], grad_gate, 0), (wide_v.at[:, pl.ds(HID, HID)], grad_up, 1), (down_v, grad_down, 2),
    ):
        moves.append(pltpu.make_async_copy(src, dst, out_sem.at[sem]))
        moves[-1].start()
    for copy in moves:
        copy.wait()


def finish(put_t, sums, back, wide, down):
    bf = jnp.bfloat16
    any_ = pl.BlockSpec(memory_space=pl.ANY)
    vm = pl.BlockSpec(memory_space=pltpu.VMEM)
    return pl.pallas_call(
        finish_kernel,
        out_shape=(
            jax.ShapeDtypeStruct((TOK, D), bf),
            jax.ShapeDtypeStruct((2, TOK), bf),
            jax.ShapeDtypeStruct((SLICE, HID), bf),
            jax.ShapeDtypeStruct((SLICE, HID), bf),
            jax.ShapeDtypeStruct((HID, SLICE), bf),
        ),
        in_specs=[vm, vm, any_, any_, any_],
        out_specs=(any_, vm, any_, any_, any_),
        scratch_shapes=[
            pltpu.VMEM((NE, CAP, D), bf),
            pltpu.VMEM((TOK, D), bf),
            pltpu.VMEM((SLICE, 2 * HID), bf),
            pltpu.VMEM((HID, SLICE), bf),
            pltpu.SemaphoreType.DMA((6,)),
            pltpu.SemaphoreType.DMA((7,)),
        ],
        compiler_params=pltpu.CompilerParams(vmem_limit_bytes=60 * 2**20),
    )(put_t, sums, back, wide, down)


def on_device(tokens, grad_out, expert_ids, combine, w_gate, w_up, w_down):
    back, _, _, put_t, sums, wide, down = exchange(
        expert_ids.T, combine.T, tokens, grad_out, w_gate[0], w_up[0], w_down[0]
    )
    grad_tokens, grad_combine, grad_gate, grad_up, grad_down = finish(put_t, sums, back, wide, down)
    return grad_tokens, grad_combine.T, grad_gate[None], grad_up[None], grad_down[None]


def solution(mesh):
    return jax.shard_map(
        on_device,
        mesh=mesh,
        in_specs=(
            P(("dp", "expert"), None),
            P(("dp", "expert"), None),
            P(("dp", "expert"), None),
            P(("dp", "expert"), None),
            P("expert", None, None),
            P("expert", None, None),
            P("expert", None, None),
        ),
        out_specs=(
            P(("dp", "expert"), None),
            P(("dp", "expert"), None),
            P("expert", "dp", None),
            P("expert", "dp", None),
            P("expert", None, "dp"),
        ),
        check_vma=False,
    )
```

```python
import jax
import jax.numpy as jnp
from jax import lax
from jax.experimental import pallas as pl
from jax.experimental.pallas import tpu as pltpu
from jax.sharding import PartitionSpec as P

MESH = pl.DeviceIdType.MESH
NX, NY, NZ, NE = 4, 4, 4, 32
CAP = 24
D, HID = 4096, 512
SLICE = D // NZ
GROUP = 8
GROUPS = NE // GROUP
ROWS = GROUP * CAP
TOK = 256
PARTNER, OWN = NE - 2, NE - 1
SC = 2048
VMEM_BYTES = 63 * 2**20
OFFSETS = (
    (1, 0), (3, 0), (0, 1), (0, 3), (1, 1), (3, 3), (1, 3), (3, 1),
    (2, 0), (0, 2), (1, 2), (3, 2), (2, 1), (2, 3), (2, 2),
)


def offset(i, core):
    dx, dy = OFFSETS[i]
    return dx + core * (dy - dx), dy + core * (dx - dy)


def expert_at(x, y, core):
    return (y % NY) * (2 * NX) + (x % NX) * 2 + core


def nt(left, right):
    return lax.dot_general(left, right, (((1,), (1,)), ((), ())), preferred_element_type=jnp.float32)


def tn(left, right):
    return lax.dot_general(left, right, (((0,), (0,)), ((), ())), preferred_element_type=jnp.float32)


def kernel(
    ids_t, weight_t, tok_h, dy_h, wg_h, wu_h, wd_h,
    back, sx, sdy, put_t, out_c, wide_h, down_h,
    tokdy, stage, out_gu, out_d, put, put0, put1, put_dy, back_c, xr, dyr, pg, pc, wg, wu, wd, xz, gz, gown, hid, dn_in, dn_rel, fa, fb,
    in_sem, out_sem, st_sem, w_sem, loc_sem, x_recv, dy_recv, x_send, dy_send, pg_recv, pg_send, pc_recv, pc_send,
    xz_recv, xz_send, gz_next, gz_prev, gz_far, gz_send, dn_recv, rel_recv, dn_send,
):
    bf, f32 = jnp.bfloat16, jnp.float32
    z = lax.axis_index("dp")
    ex = lax.axis_index("expert")
    c = ex % 2
    x = (ex // 2) % NX
    y = ex // (2 * NX)

    loads = [
        pltpu.make_async_copy(wg_h, wg, w_sem.at[0]),
        pltpu.make_async_copy(wu_h, wu, w_sem.at[1]),
        pltpu.make_async_copy(wd_h, wd, w_sem.at[2]),
        pltpu.make_async_copy(sx.at[OWN], xr.at[OWN], loc_sem.at[0]),
        pltpu.make_async_copy(sdy.at[OWN], dyr.at[OWN], loc_sem.at[1]),
    ]

    barrier = pltpu.get_barrier_semaphore()

    def greet(k, carry):
        pl.semaphore_signal(barrier, inc=1, device_id=(z, (ex + k) % NE), device_id_type=MESH)
        return carry

    lax.fori_loop(1, NE, greet, 0)
    for j in range(1, NZ):
        pl.semaphore_signal(barrier, inc=1, device_id=((z + j) % NZ, ex), device_id_type=MESH)
    fetch = [pltpu.make_async_copy(tok_h, tokdy.at[0], in_sem.at[0]), pltpu.make_async_copy(dy_h, tokdy.at[1], in_sem.at[1])]
    for load in fetch + loads[:3]:
        load.start()

    ids = [ids_t[k : k + 1, :].astype(f32) for k in range(2)]
    weight = weight_t[...].astype(f32)
    position = lax.broadcasted_iota(jnp.int32, (NE, TOK), 0)
    label = jnp.where(position == OWN, ex, ex + 1 - 2 * c)
    for n in range(PARTNER):
        dx, dy = offset(n // 2, c)
        label = jnp.where(position == n, expert_at(x + dx, y + dy, n % 2), label)
    label = label.astype(f32)
    position = position.astype(f32)
    hits = [(label == ids[k]).astype(f32) for k in range(2)]
    first = lax.broadcasted_iota(jnp.int32, (TOK, TOK), 0)
    second = lax.broadcasted_iota(jnp.int32, (TOK, TOK), 1)
    before = (first < second).astype(f32).astype(bf)
    earlier = jnp.dot((hits[0] + hits[1]).astype(bf), before, preferred_element_type=f32)
    places = [jnp.sum((position * CAP + earlier) * hits[k], axis=0, keepdims=True) for k in range(2)]
    index = lax.broadcasted_iota(jnp.int32, (NE * CAP, TOK), 0).astype(f32)
    put_k = [(index == places[k]).astype(f32) for k in range(2)]
    put[...] = (put_k[0] + put_k[1]).astype(bf)
    put0[...] = put_k[0].astype(bf)
    put1[...] = put_k[1].astype(bf)
    put_dy[...] = (put_k[0] * weight[0:1] + put_k[1] * weight[1:2]).astype(bf)

    def to_expert(src, dst, send, recv, n):
        if n == PARTNER:
            to, slot = ex + 1 - 2 * c, PARTNER
        else:
            i, core = n // 2, n % 2
            dx, dy = offset(i, c)
            to, slot = expert_at(x + dx, y + dy, core), 2 * i + c
        return pltpu.make_async_remote_copy(
            src_ref=src.at[n], dst_ref=dst.at[slot], send_sem=send, recv_sem=recv.at[n // GROUP],
            device_id=(z, to), device_id_type=MESH,
        )

    kinds = ((put, sx, xr, x_send, x_recv), (put_dy, sdy, dyr, dy_send, dy_recv))

    def stage_out(step, h):
        which, g = divmod(step, GROUPS)
        kk = pl.ds(pl.multiple_of(h * SC, SC), SC)
        return pltpu.make_async_copy(
            stage.at[h], kinds[which][1].at[pl.ds(GROUP * g, GROUP), :, kk], st_sem.at[h]
        )

    def leave(step):
        which, g = divmod(step, GROUPS)
        _, src, dst, send, recv = kinds[which]
        for n in range(GROUP * g, GROUP * (g + 1)):
            if n == OWN:
                loads[3 + which].start()
            else:
                to_expert(src, dst, send, recv, n).start()

    for step in range(2 * GROUPS):
        which, g = divmod(step, GROUPS)
        if g == 0:
            fetch[which].wait()

        def lay_out(h, carry):
            if step > 0:
                stage_out(step - 1, h).wait()
            kk = pl.ds(pl.multiple_of(h * SC, SC), SC)
            made = jnp.dot(kinds[which][0][pl.ds(g * ROWS, ROWS), :], tokdy[which, :, kk], preferred_element_type=f32)
            stage[h] = made.reshape(GROUP, CAP, SC).astype(bf)
            stage_out(step, h).start()
            return carry

        lax.fori_loop(0, D // SC, lay_out, 0)
        if step == 1:
            pl.semaphore_wait(barrier, NE - 1 + NZ - 1)
        if step > 0:
            leave(step - 1)
    for h in range(D // SC):
        stage_out(2 * GROUPS - 1, h).wait()
    leave(2 * GROUPS - 1)

    def wait_recv(dst, sem):
        pltpu.make_async_remote_copy(
            src_ref=dst, dst_ref=dst, send_sem=x_send, recv_sem=sem,
            device_id=(z, (ex + 1) % NE), device_id_type=MESH,
        ).wait_recv()

    def wait_send(src, sem):
        pltpu.make_async_remote_copy(
            src_ref=src, dst_ref=src, send_sem=sem, recv_sem=x_recv.at[0],
            device_id=(z, (ex + 1) % NE), device_id_type=MESH,
        ).wait_send()

    def arrive(dst, recv, own, g):
        @pl.when(g == GROUPS - 1)
        def _():
            loads[own].wait()
            wait_recv(dst.at[pl.ds(NE - GROUP, GROUP - 1)], recv.at[GROUPS - 1])

        @pl.when(g < GROUPS - 1)
        def _():
            wait_recv(dst.at[pl.ds(GROUP * g, GROUP)], recv.at[g])

    def over_z(src, dst, send, recv, j):
        return pltpu.make_async_remote_copy(
            src_ref=src, dst_ref=dst, send_sem=send, recv_sem=recv,
            device_id=((z + j) % NZ, ex), device_id_type=MESH,
        )

    def give_back(slot):
        if slot == OWN:
            return [
                pltpu.make_async_copy(pg.at[OWN], back.at[OWN], loc_sem.at[2]),
                pltpu.make_async_copy(pc.at[OWN], back_c.at[OWN], loc_sem.at[3]),
            ]
        if slot == PARTNER:
            to, n = ex + 1 - 2 * c, PARTNER
        else:
            i, core = slot // 2, slot % 2
            dx, dy = offset(i, core)
            to, n = expert_at(x - dx, y - dy, core), 2 * i + c
        return [
            pltpu.make_async_remote_copy(
                src_ref=src.at[slot], dst_ref=dst.at[n], send_sem=send, recv_sem=recv,
                device_id=(z, to), device_id_type=MESH,
            )
            for src, dst, send, recv in ((pg, back, pg_send, pg_recv), (pc, back_c, pc_send, pc_recv))
        ]

    for k in range(NE * CAP // TOK):
        part = pl.ds(k * TOK, TOK)
        put_t[:, part] = put[part, :].astype(f32).T.astype(bf)

    for load in loads[:3]:
        load.wait()

    def pass_on(g):
        rows = pl.ds(pl.multiple_of(g * ROWS, ROWS), ROWS)
        wait_recv(gz.at[0, rows], gz_next.at[g])
        low = pl.ds(pl.multiple_of(g * ROWS, ROWS // 2), ROWS // 2)
        over_z(gz.at[0, low], gz.at[1, low], gz_send, gz_far, 1).start()
        wait_recv(gz.at[2, rows], gz_prev.at[g])
        high = pl.ds(pl.multiple_of(g * ROWS + ROWS // 2, ROWS // 2), ROWS // 2)
        over_z(gz.at[2, high], gz.at[1, high], gz_send, gz_far, 3).start()

    def spread(g, carry):
        base = pl.multiple_of(GROUP * g, GROUP)
        arrive(xr, x_recv, 3, g)
        for j in (2, 1, 3):
            cols = pl.ds(pl.multiple_of((z + j) % NZ * SLICE, SLICE), SLICE)
            over_z(xr.at[pl.ds(base, GROUP), :, cols], xz.at[j - 1, pl.ds(base, GROUP)], xz_send, xz_recv, j).start()
        return carry

    lax.fori_loop(0, GROUPS, spread, 0)

    KC = 1024

    def group_step(g, carry):
        base = pl.multiple_of(GROUP * g, GROUP)
        rows = pl.ds(pl.multiple_of(g * ROWS, ROWS), ROWS)
        fa[...] = jnp.zeros_like(fa)
        fb[...] = jnp.zeros_like(fb)

        def forward(k, cc):
            kk = pl.ds(pl.multiple_of(k * KC, KC), KC)
            xk = xr[pl.ds(base, GROUP), :, kk].reshape(ROWS, KC)
            fa[...] += jnp.dot(xk, wg[kk, :], preferred_element_type=jnp.float32)
            fb[...] += jnp.dot(xk, wu[kk, :], preferred_element_type=jnp.float32)
            return cc

        lax.fori_loop(0, D // KC, forward, 0)
        gate = fa[...]
        upper = fb[...]
        sigma = 1.0 / (1.0 + jnp.exp(-gate))
        swish = gate * sigma
        hidden = (swish * upper).astype(jnp.bfloat16)
        hid[rows, :] = hidden
        fa[...] = upper * sigma * (1.0 + gate * (1.0 - sigma))
        fb[...] = swish

        @pl.when(g >= 1)
        def _():
            pass_on(g - 1)

        arrive(dyr, dy_recv, 4, g)

        def backward(k, hg):
            kk = pl.ds(pl.multiple_of(k * KC, KC), KC)
            dk = dyr[pl.ds(base, GROUP), :, kk].reshape(ROWS, KC)
            return hg + nt(dk, wd[:, kk])

        hg = lax.fori_loop(0, D // KC, backward, jnp.zeros((ROWS, HID), jnp.float32))
        gown[rows, pl.ds(0, HID)] = (hg * fa[...]).astype(jnp.bfloat16)
        gown[rows, pl.ds(HID, HID)] = (hg * fb[...]).astype(jnp.bfloat16)
        over_z(gown.at[rows], gz.at[0, rows], gz_send, gz_next.at[g], 1).start()
        over_z(gown.at[rows], gz.at[2, rows], gz_send, gz_prev.at[g], 3).start()
        total = jnp.sum(hid[rows, :].astype(jnp.float32) * hg, axis=1, keepdims=True)
        total = jnp.broadcast_to(total, (ROWS, 128))
        high = total.astype(jnp.bfloat16).astype(jnp.float32)
        lane = lax.broadcasted_iota(jnp.int32, (ROWS, 128), 1)
        pc[pl.ds(base, GROUP)] = (
            jnp.where(lane < 64, high, total - high).reshape(GROUP, CAP, 128).astype(jnp.bfloat16)
        )

        def inward(k, cc):
            kk = pl.ds(pl.multiple_of(k * KC, KC), KC)
            part = nt(gown[rows, pl.ds(0, HID)], wg[kk, :]) + nt(gown[rows, pl.ds(HID, HID)], wu[kk, :])
            pg[pl.ds(base, GROUP), :, kk] = part.reshape(GROUP, CAP, KC).astype(jnp.bfloat16)
            return cc

        lax.fori_loop(0, D // KC, inward, 0)
        for done in range(GROUPS):

            @pl.when(g == done)
            def _():
                for slot in range(GROUP * done, GROUP * (done + 1)):
                    for copy in give_back(slot):
                        copy.start()

        return carry

    lax.fori_loop(0, GROUPS, group_step, 0)

    pass_on(GROUPS - 1)

    def down_part(j):
        cols = pl.ds(pl.multiple_of((z + j) % NZ * SLICE, SLICE), SLICE)
        total = jnp.zeros((HID, SLICE), jnp.float32)

        def add(g, total):
            rows = pl.ds(pl.multiple_of(g * ROWS, ROWS), ROWS)
            dk = dyr[pl.ds(pl.multiple_of(GROUP * g, GROUP), GROUP), :, cols].reshape(ROWS, SLICE)
            return total + tn(hid[rows, :], dk)

        return lax.fori_loop(0, GROUPS, add, total)

    half = HID // 2
    low, high = pl.ds(0, half), pl.ds(half, half)

    def dn_out(h, j):
        return tokdy.at[h, :, pl.ds((j - 1) * SLICE, SLICE)]

    def make_down(j):
        part = down_part(j).astype(bf)
        dn_out(0, j)[...] = part[:half]
        dn_out(1, j)[...] = part[half:]

    make_down(2)
    over_z(dn_out(0, 2), dn_rel.at[0], dn_send, rel_recv.at[0], 1).start()
    over_z(dn_out(1, 2), dn_rel.at[1], dn_send, rel_recv.at[1], 3).start()
    make_down(1)
    over_z(dn_out(1, 1), dn_in.at[0, high], dn_send, dn_recv, 1).start()
    make_down(3)
    over_z(dn_out(0, 3), dn_in.at[1, low], dn_send, dn_recv, 3).start()

    wait_recv(xz, xz_recv)
    wait_recv(gz.at[1], gz_far)
    CB = 256

    def wide(k, carry):
        off = pl.multiple_of(k * CB, CB)
        mine = pl.ds(pl.multiple_of(z * SLICE + off, CB), CB)
        total = tn(xr[:, :, mine].reshape(NE * CAP, CB), gown[...])
        for j in range(NZ - 1):
            total += tn(xz[j, :, :, pl.ds(off, CB)].reshape(NE * CAP, CB), gz[j])
        out_gu[pl.ds(off, CB), :] = total.astype(bf)
        return carry

    lax.fori_loop(0, SLICE // CB, wide, 0)
    wide_out = pltpu.make_async_copy(out_gu, wide_h, out_sem.at[0])
    wide_out.start()

    for h, j in ((0, 1), (1, 3)):
        wait_recv(dn_rel.at[h], rel_recv.at[h])
        dn_out(h, j)[...] = (dn_out(h, j)[...].astype(f32) + dn_rel[h].astype(f32)).astype(bf)
        over_z(dn_out(h, j), dn_in.at[h, high if h else low], dn_send, dn_recv, j).start()
    own = down_part(0)
    wait_recv(dn_in, dn_recv)
    for j in range(2):
        own += dn_in[j].astype(f32)
    out_d[...] = own.astype(bf)
    down_out = pltpu.make_async_copy(out_d, down_h, out_sem.at[1])
    down_out.start()

    most = pl.ds(0, NE - 1)
    wait_send(sx.at[most], x_send)
    wait_send(sdy.at[most], dy_send)
    wait_send(xz, xz_send)
    wait_send(gz, gz_send)
    wait_send(tokdy.at[:, :, pl.ds(0, (NZ - 1) * SLICE)], dn_send)
    wait_send(pg.at[most], pg_send)
    wait_send(pc.at[most], pc_send)
    for copy in give_back(OWN):
        copy.wait()
    wait_recv(back_c.at[most], pc_recv)
    sums = back_c[...].reshape(NE * CAP, 128)
    for k, rows in ((0, put0), (1, put1)):
        both = tn(sums, rows[...])
        out_c[k : k + 1, :] = (both[0:1] + both[64:65]) / weight_t[k : k + 1, :].astype(f32)
    wait_recv(back.at[most], pg_recv)
    wide_out.wait()
    down_out.wait()


def exchange(ids_t, weight_t, tokens, grad_out, w_gate, w_up, w_down):
    bf, f32 = jnp.bfloat16, jnp.float32
    any_ = pl.BlockSpec(memory_space=pl.ANY)
    vm = pl.BlockSpec(memory_space=pltpu.VMEM)
    dma = pltpu.SemaphoreType.DMA
    return pl.pallas_call(
        kernel,
        out_shape=(
            jax.ShapeDtypeStruct((NE, CAP, D), bf),
            jax.ShapeDtypeStruct((NE, CAP, D), bf),
            jax.ShapeDtypeStruct((NE, CAP, D), bf),
            jax.ShapeDtypeStruct((TOK, NE * CAP), bf),
            jax.ShapeDtypeStruct((2, TOK), f32),
            jax.ShapeDtypeStruct((SLICE, 2 * HID), bf),
            jax.ShapeDtypeStruct((HID, SLICE), bf),
        ),
        in_specs=[vm] * 2 + [any_] * 5,
        out_specs=(any_, any_, any_, vm, vm, any_, any_),
        scratch_shapes=[
            pltpu.VMEM((2, TOK, D), bf),
            pltpu.VMEM((D // SC, GROUP, CAP, SC), bf),
            pltpu.VMEM((SLICE, 2 * HID), bf),
            pltpu.VMEM((HID, SLICE), bf),
            pltpu.VMEM((NE * CAP, TOK), bf),
            pltpu.VMEM((NE * CAP, TOK), bf),
            pltpu.VMEM((NE * CAP, TOK), bf),
            pltpu.VMEM((NE * CAP, TOK), bf),
            pltpu.VMEM((NE, CAP, 128), bf),
            pltpu.VMEM((NE, CAP, D), bf),
            pltpu.VMEM((NE, CAP, D), bf),
            pltpu.VMEM((NE, CAP, D), bf),
            pltpu.VMEM((NE, CAP, 128), bf),
            pltpu.VMEM((D, HID), bf),
            pltpu.VMEM((D, HID), bf),
            pltpu.VMEM((HID, D), bf),
            pltpu.VMEM((NZ - 1, NE, CAP, SLICE), bf),
            pltpu.VMEM((NZ - 1, NE * CAP, 2 * HID), bf),
            pltpu.VMEM((NE * CAP, 2 * HID), bf),
            pltpu.VMEM((NE * CAP, HID), bf),
            pltpu.VMEM((2, HID, SLICE), bf),
            pltpu.VMEM((2, HID // 2, SLICE), bf),
            pltpu.VMEM((ROWS, HID), f32),
            pltpu.VMEM((ROWS, HID), f32),
            dma((2,)), dma((2,)), dma((2,)), dma((3,)), dma((4,)), dma((GROUPS,)), dma((GROUPS,)),
        ] + [dma] * 6 + [dma] * 2 + [dma((GROUPS,)), dma((GROUPS,)), dma, dma, dma, dma((2,)), dma],
        compiler_params=pltpu.CompilerParams(
            collective_id=0, has_side_effects=True, vmem_limit_bytes=VMEM_BYTES
        ),
    )(ids_t, weight_t, tokens, grad_out, w_gate, w_up, w_down)


def finish_kernel(
    put_t, sums, back, wide, down, grad_tokens, grad_combine, grad_gate, grad_up, grad_down,
    rows, made, wide_v, down_v, load_sem, out_sem,
):
    steps = 4
    width = D // steps
    loads = [
        pltpu.make_async_copy(back.at[:, :, pl.ds(k * width, width)], rows.at[:, :, pl.ds(k * width, width)], load_sem.at[k])
        for k in range(steps)
    ]
    loads.append(pltpu.make_async_copy(wide, wide_v, load_sem.at[steps]))
    loads.append(pltpu.make_async_copy(down, down_v, load_sem.at[steps + 1]))
    for copy in loads:
        copy.start()
    moves = []
    grad_combine[...] = sums[...].astype(jnp.bfloat16)
    for k in range(steps):
        kk = pl.ds(k * width, width)
        loads[k].wait()
        block = rows[:, :, kk].reshape(NE * CAP, width)
        made[:, kk] = jnp.dot(put_t[...], block, preferred_element_type=jnp.float32).astype(jnp.bfloat16)
        moves.append(pltpu.make_async_copy(made.at[:, kk], grad_tokens.at[:, kk], out_sem.at[3 + k]))
        moves[-1].start()
    loads[steps].wait()
    loads[steps + 1].wait()
    for src, dst, sem in (
        (wide_v.at[:, pl.ds(0, HID)], grad_gate, 0), (wide_v.at[:, pl.ds(HID, HID)], grad_up, 1), (down_v, grad_down, 2),
    ):
        moves.append(pltpu.make_async_copy(src, dst, out_sem.at[sem]))
        moves[-1].start()
    for copy in moves:
        copy.wait()


def finish(put_t, sums, back, wide, down):
    bf = jnp.bfloat16
    any_ = pl.BlockSpec(memory_space=pl.ANY)
    vm = pl.BlockSpec(memory_space=pltpu.VMEM)
    return pl.pallas_call(
        finish_kernel,
        out_shape=(
            jax.ShapeDtypeStruct((TOK, D), bf),
            jax.ShapeDtypeStruct((2, TOK), bf),
            jax.ShapeDtypeStruct((SLICE, HID), bf),
            jax.ShapeDtypeStruct((SLICE, HID), bf),
            jax.ShapeDtypeStruct((HID, SLICE), bf),
        ),
        in_specs=[vm, vm, any_, any_, any_],
        out_specs=(any_, vm, any_, any_, any_),
        scratch_shapes=[
            pltpu.VMEM((NE, CAP, D), bf),
            pltpu.VMEM((TOK, D), bf),
            pltpu.VMEM((SLICE, 2 * HID), bf),
            pltpu.VMEM((HID, SLICE), bf),
            pltpu.SemaphoreType.DMA((6,)),
            pltpu.SemaphoreType.DMA((7,)),
        ],
        compiler_params=pltpu.CompilerParams(vmem_limit_bytes=60 * 2**20),
    )(put_t, sums, back, wide, down)


def on_device(tokens, grad_out, expert_ids, combine, w_gate, w_up, w_down):
    back, _, _, put_t, sums, wide, down = exchange(
        expert_ids.T, combine.T, tokens, grad_out, w_gate[0], w_up[0], w_down[0]
    )
    grad_tokens, grad_combine, grad_gate, grad_up, grad_down = finish(put_t, sums, back, wide, down)
    return grad_tokens, grad_combine.T, grad_gate[None], grad_up[None], grad_down[None]


def solution(mesh):
    return jax.shard_map(
        on_device,
        mesh=mesh,
        in_specs=(
            P(("dp", "expert"), None),
            P(("dp", "expert"), None),
            P(("dp", "expert"), None),
            P(("dp", "expert"), None),
            P("expert", None, None),
            P("expert", None, None),
            P("expert", None, None),
        ),
        out_specs=(
            P(("dp", "expert"), None),
            P(("dp", "expert"), None),
            P("expert", "dp", None),
            P("expert", "dp", None),
            P("expert", None, "dp"),
        ),
        check_vma=False,
    )
```

```python
import jax
import jax.numpy as jnp
from jax import lax
from jax.experimental import pallas as pl
from jax.experimental.pallas import tpu as pltpu
from jax.sharding import PartitionSpec as P

MESH = pl.DeviceIdType.MESH
NX, NY, NZ, NE = 4, 4, 4, 32
CAP = 24
D, HID = 4096, 512
SLICE = D // NZ
GROUP = 8
GROUPS = NE // GROUP
ROWS = GROUP * CAP
EARLY = NE - GROUP
TOK = 256
PARTNER, OWN = NE - 2, NE - 1
SC = 2048
VMEM_BYTES = 63 * 2**20
OFFSETS = (
    (1, 0), (3, 0), (0, 1), (0, 3), (1, 1), (3, 3), (1, 3), (3, 1),
    (2, 0), (0, 2), (1, 2), (3, 2), (2, 1), (2, 3), (2, 2),
)


def offset(i, core):
    dx, dy = OFFSETS[i]
    return dx + core * (dy - dx), dy + core * (dx - dy)


def expert_at(x, y, core):
    return (y % NY) * (2 * NX) + (x % NX) * 2 + core


def nt(left, right):
    return lax.dot_general(left, right, (((1,), (1,)), ((), ())), preferred_element_type=jnp.float32)


def tn(left, right):
    return lax.dot_general(left, right, (((0,), (0,)), ((), ())), preferred_element_type=jnp.float32)


def kernel(
    ids_t, weight_t, tok_h, dy_h, wg_h, wu_h, wd_h,
    back, sx, sdy, early_h, put_last, out_c, wide_h, down_h,
    tokdy, stage, out_gu, out_d, put, put0, put1, put_dy, back_c, xr, dyr, pg, pc, wg, wu, wd, xz, gz, gown, hid, dn_in, dn_rel, fa, fb,
    in_sem, out_sem, early_sem, st_sem, w_sem, loc_sem, x_recv, dy_recv, x_send, dy_send, pg_recv, pg_send, pc_recv, pc_send,
    xz_recv, xz_send, gz_next, gz_prev, gz_far, gz_send, dn_recv, rel_recv, dn_send,
):
    bf, f32 = jnp.bfloat16, jnp.float32
    z = lax.axis_index("dp")
    ex = lax.axis_index("expert")
    c = ex % 2
    x = (ex // 2) % NX
    y = ex // (2 * NX)

    loads = [
        pltpu.make_async_copy(wg_h, wg, w_sem.at[0]),
        pltpu.make_async_copy(wu_h, wu, w_sem.at[1]),
        pltpu.make_async_copy(wd_h, wd, w_sem.at[2]),
        pltpu.make_async_copy(sx.at[OWN], xr.at[OWN], loc_sem.at[0]),
        pltpu.make_async_copy(sdy.at[OWN], dyr.at[OWN], loc_sem.at[1]),
    ]

    barrier = pltpu.get_barrier_semaphore()

    def greet(k, carry):
        pl.semaphore_signal(barrier, inc=1, device_id=(z, (ex + k) % NE), device_id_type=MESH)
        return carry

    lax.fori_loop(1, NE, greet, 0)
    for j in range(1, NZ):
        pl.semaphore_signal(barrier, inc=1, device_id=((z + j) % NZ, ex), device_id_type=MESH)
    fetch = [pltpu.make_async_copy(tok_h, tokdy.at[0], in_sem.at[0]), pltpu.make_async_copy(dy_h, tokdy.at[1], in_sem.at[1])]
    for load in fetch + loads[:3]:
        load.start()

    ids = [ids_t[k : k + 1, :].astype(f32) for k in range(2)]
    weight = weight_t[...].astype(f32)
    position = lax.broadcasted_iota(jnp.int32, (NE, TOK), 0)
    label = jnp.where(position == OWN, ex, ex + 1 - 2 * c)
    for n in range(PARTNER):
        dx, dy = offset(n // 2, c)
        label = jnp.where(position == n, expert_at(x + dx, y + dy, n % 2), label)
    label = label.astype(f32)
    position = position.astype(f32)
    hits = [(label == ids[k]).astype(f32) for k in range(2)]
    first = lax.broadcasted_iota(jnp.int32, (TOK, TOK), 0)
    second = lax.broadcasted_iota(jnp.int32, (TOK, TOK), 1)
    before = (first < second).astype(f32).astype(bf)
    earlier = jnp.dot((hits[0] + hits[1]).astype(bf), before, preferred_element_type=f32)
    places = [jnp.sum((position * CAP + earlier) * hits[k], axis=0, keepdims=True) for k in range(2)]
    index = lax.broadcasted_iota(jnp.int32, (NE * CAP, TOK), 0).astype(f32)
    put_k = [(index == places[k]).astype(f32) for k in range(2)]
    put[...] = (put_k[0] + put_k[1]).astype(bf)
    put0[...] = put_k[0].astype(bf)
    put1[...] = put_k[1].astype(bf)
    put_dy[...] = (put_k[0] * weight[0:1] + put_k[1] * weight[1:2]).astype(bf)

    def to_expert(src, dst, send, recv, n):
        if n == PARTNER:
            to, slot = ex + 1 - 2 * c, PARTNER
        else:
            i, core = n // 2, n % 2
            dx, dy = offset(i, c)
            to, slot = expert_at(x + dx, y + dy, core), 2 * i + c
        return pltpu.make_async_remote_copy(
            src_ref=src.at[n], dst_ref=dst.at[slot], send_sem=send, recv_sem=recv.at[n // GROUP],
            device_id=(z, to), device_id_type=MESH,
        )

    kinds = ((put, sx, xr, x_send, x_recv), (put_dy, sdy, dyr, dy_send, dy_recv))

    def stage_out(step, h):
        which, g = divmod(step, GROUPS)
        kk = pl.ds(pl.multiple_of(h * SC, SC), SC)
        return pltpu.make_async_copy(
            stage.at[h], kinds[which][1].at[pl.ds(GROUP * g, GROUP), :, kk], st_sem.at[h]
        )

    def leave(step):
        which, g = divmod(step, GROUPS)
        _, src, dst, send, recv = kinds[which]
        for n in range(GROUP * g, GROUP * (g + 1)):
            if n == OWN:
                loads[3 + which].start()
            else:
                to_expert(src, dst, send, recv, n).start()

    for step in range(2 * GROUPS):
        which, g = divmod(step, GROUPS)
        if g == 0:
            fetch[which].wait()

        def lay_out(h, carry):
            if step > 0:
                stage_out(step - 1, h).wait()
            kk = pl.ds(pl.multiple_of(h * SC, SC), SC)
            made = jnp.dot(kinds[which][0][pl.ds(g * ROWS, ROWS), :], tokdy[which, :, kk], preferred_element_type=f32)
            stage[h] = made.reshape(GROUP, CAP, SC).astype(bf)
            stage_out(step, h).start()
            return carry

        lax.fori_loop(0, D // SC, lay_out, 0)
        if step == 1:
            pl.semaphore_wait(barrier, NE - 1 + NZ - 1)
        if step > 0:
            leave(step - 1)
    for h in range(D // SC):
        stage_out(2 * GROUPS - 1, h).wait()
    leave(2 * GROUPS - 1)

    def wait_recv(dst, sem):
        pltpu.make_async_remote_copy(
            src_ref=dst, dst_ref=dst, send_sem=x_send, recv_sem=sem,
            device_id=(z, (ex + 1) % NE), device_id_type=MESH,
        ).wait_recv()

    def wait_send(src, sem):
        pltpu.make_async_remote_copy(
            src_ref=src, dst_ref=src, send_sem=sem, recv_sem=x_recv.at[0],
            device_id=(z, (ex + 1) % NE), device_id_type=MESH,
        ).wait_send()

    def arrive(dst, recv, own, g):
        @pl.when(g == GROUPS - 1)
        def _():
            loads[own].wait()
            wait_recv(dst.at[pl.ds(NE - GROUP, GROUP - 1)], recv.at[GROUPS - 1])

        @pl.when(g < GROUPS - 1)
        def _():
            wait_recv(dst.at[pl.ds(GROUP * g, GROUP)], recv.at[g])

    def over_z(src, dst, send, recv, j):
        return pltpu.make_async_remote_copy(
            src_ref=src, dst_ref=dst, send_sem=send, recv_sem=recv,
            device_id=((z + j) % NZ, ex), device_id_type=MESH,
        )

    def give_back(slot):
        if slot == OWN:
            return [
                pltpu.make_async_copy(pg.at[OWN], back.at[OWN], loc_sem.at[2]),
                pltpu.make_async_copy(pc.at[OWN], back_c.at[OWN], loc_sem.at[3]),
            ]
        if slot == PARTNER:
            to, n = ex + 1 - 2 * c, PARTNER
        else:
            i, core = slot // 2, slot % 2
            dx, dy = offset(i, core)
            to, n = expert_at(x - dx, y - dy, core), 2 * i + c
        return [
            pltpu.make_async_remote_copy(
                src_ref=src.at[slot], dst_ref=dst.at[n], send_sem=send, recv_sem=recv,
                device_id=(z, to), device_id_type=MESH,
            )
            for src, dst, send, recv in ((pg, back, pg_send, pg_recv.at[slot // GROUP]), (pc, back_c, pc_send, pc_recv))
        ]

    put_last[...] = put[pl.ds(EARLY * CAP, ROWS), :]

    for load in loads[:3]:
        load.wait()

    def pass_on(g):
        rows = pl.ds(pl.multiple_of(g * ROWS, ROWS), ROWS)
        wait_recv(gz.at[0, rows], gz_next.at[g])
        low = pl.ds(pl.multiple_of(g * ROWS, ROWS // 2), ROWS // 2)
        over_z(gz.at[0, low], gz.at[1, low], gz_send, gz_far, 1).start()
        wait_recv(gz.at[2, rows], gz_prev.at[g])
        high = pl.ds(pl.multiple_of(g * ROWS + ROWS // 2, ROWS // 2), ROWS // 2)
        over_z(gz.at[2, high], gz.at[1, high], gz_send, gz_far, 3).start()

    def spread(g, carry):
        base = pl.multiple_of(GROUP * g, GROUP)
        arrive(xr, x_recv, 3, g)
        for j in (2, 1, 3):
            cols = pl.ds(pl.multiple_of((z + j) % NZ * SLICE, SLICE), SLICE)
            over_z(xr.at[pl.ds(base, GROUP), :, cols], xz.at[j - 1, pl.ds(base, GROUP)], xz_send, xz_recv, j).start()
        return carry

    lax.fori_loop(0, GROUPS, spread, 0)

    KC = 1024

    def group_step(g, carry):
        base = pl.multiple_of(GROUP * g, GROUP)
        rows = pl.ds(pl.multiple_of(g * ROWS, ROWS), ROWS)
        fa[...] = jnp.zeros_like(fa)
        fb[...] = jnp.zeros_like(fb)

        def forward(k, cc):
            kk = pl.ds(pl.multiple_of(k * KC, KC), KC)
            xk = xr[pl.ds(base, GROUP), :, kk].reshape(ROWS, KC)
            fa[...] += jnp.dot(xk, wg[kk, :], preferred_element_type=jnp.float32)
            fb[...] += jnp.dot(xk, wu[kk, :], preferred_element_type=jnp.float32)
            return cc

        lax.fori_loop(0, D // KC, forward, 0)
        gate = fa[...]
        upper = fb[...]
        sigma = 1.0 / (1.0 + jnp.exp(-gate))
        swish = gate * sigma
        hidden = (swish * upper).astype(jnp.bfloat16)
        hid[rows, :] = hidden
        fa[...] = upper * sigma * (1.0 + gate * (1.0 - sigma))
        fb[...] = swish

        @pl.when(g >= 1)
        def _():
            pass_on(g - 1)

        arrive(dyr, dy_recv, 4, g)

        def backward(k, hg):
            kk = pl.ds(pl.multiple_of(k * KC, KC), KC)
            dk = dyr[pl.ds(base, GROUP), :, kk].reshape(ROWS, KC)
            return hg + nt(dk, wd[:, kk])

        hg = lax.fori_loop(0, D // KC, backward, jnp.zeros((ROWS, HID), jnp.float32))
        gown[rows, pl.ds(0, HID)] = (hg * fa[...]).astype(jnp.bfloat16)
        gown[rows, pl.ds(HID, HID)] = (hg * fb[...]).astype(jnp.bfloat16)
        over_z(gown.at[rows], gz.at[0, rows], gz_send, gz_next.at[g], 1).start()
        over_z(gown.at[rows], gz.at[2, rows], gz_send, gz_prev.at[g], 3).start()
        total = jnp.sum(hid[rows, :].astype(jnp.float32) * hg, axis=1, keepdims=True)
        total = jnp.broadcast_to(total, (ROWS, 128))
        high = total.astype(jnp.bfloat16).astype(jnp.float32)
        lane = lax.broadcasted_iota(jnp.int32, (ROWS, 128), 1)
        pc[pl.ds(base, GROUP)] = (
            jnp.where(lane < 64, high, total - high).reshape(GROUP, CAP, 128).astype(jnp.bfloat16)
        )

        def inward(k, cc):
            kk = pl.ds(pl.multiple_of(k * KC, KC), KC)
            part = nt(gown[rows, pl.ds(0, HID)], wg[kk, :]) + nt(gown[rows, pl.ds(HID, HID)], wu[kk, :])
            pg[pl.ds(base, GROUP), :, kk] = part.reshape(GROUP, CAP, KC).astype(jnp.bfloat16)
            return cc

        lax.fori_loop(0, D // KC, inward, 0)
        for done in range(GROUPS):

            @pl.when(g == done)
            def _():
                for slot in range(GROUP * done, GROUP * (done + 1)):
                    for copy in give_back(slot):
                        copy.start()

        return carry

    lax.fori_loop(0, GROUPS, group_step, 0)

    pass_on(GROUPS - 1)

    def down_part(j):
        cols = pl.ds(pl.multiple_of((z + j) % NZ * SLICE, SLICE), SLICE)
        total = jnp.zeros((HID, SLICE), jnp.float32)

        def add(g, total):
            rows = pl.ds(pl.multiple_of(g * ROWS, ROWS), ROWS)
            dk = dyr[pl.ds(pl.multiple_of(GROUP * g, GROUP), GROUP), :, cols].reshape(ROWS, SLICE)
            return total + tn(hid[rows, :], dk)

        return lax.fori_loop(0, GROUPS, add, total)

    half = HID // 2
    low, high = pl.ds(0, half), pl.ds(half, half)

    def dn_out(h, j):
        return tokdy.at[h, :, pl.ds((j - 1) * SLICE, SLICE)]

    def make_down(j):
        part = down_part(j).astype(bf)
        dn_out(0, j)[...] = part[:half]
        dn_out(1, j)[...] = part[half:]

    make_down(2)
    over_z(dn_out(0, 2), dn_rel.at[0], dn_send, rel_recv.at[0], 1).start()
    over_z(dn_out(1, 2), dn_rel.at[1], dn_send, rel_recv.at[1], 3).start()
    make_down(1)
    over_z(dn_out(1, 1), dn_in.at[0, high], dn_send, dn_recv, 1).start()
    make_down(3)
    over_z(dn_out(0, 3), dn_in.at[1, low], dn_send, dn_recv, 3).start()

    wait_recv(xz, xz_recv)
    wait_recv(gz.at[1], gz_far)
    CB = 256

    def wide(k, carry):
        off = pl.multiple_of(k * CB, CB)
        mine = pl.ds(pl.multiple_of(z * SLICE + off, CB), CB)
        total = tn(xr[:, :, mine].reshape(NE * CAP, CB), gown[...])
        for j in range(NZ - 1):
            total += tn(xz[j, :, :, pl.ds(off, CB)].reshape(NE * CAP, CB), gz[j])
        out_gu[pl.ds(off, CB), :] = total.astype(bf)
        return carry

    lax.fori_loop(0, SLICE // CB, wide, 0)
    wide_out = pltpu.make_async_copy(out_gu, wide_h, out_sem.at[0])
    wide_out.start()

    for h, j in ((0, 1), (1, 3)):
        wait_recv(dn_rel.at[h], rel_recv.at[h])
        dn_out(h, j)[...] = (dn_out(h, j)[...].astype(f32) + dn_rel[h].astype(f32)).astype(bf)
        over_z(dn_out(h, j), dn_in.at[h, high if h else low], dn_send, dn_recv, j).start()
    own = down_part(0)

    wait_send(xz, xz_send)
    wait_send(gz, gz_send)
    for g in range(GROUPS - 1):
        part = pl.ds(GROUP * g, GROUP)
        wait_recv(back.at[part], pg_recv.at[g])
        pltpu.make_async_copy(back.at[part], xr.at[part], st_sem.at[0]).start()
        pltpu.make_async_copy(back.at[part], xr.at[part], st_sem.at[0]).wait()
    early_out = []
    for j in range(D // SLICE):
        cols = pl.ds(j * SLICE, SLICE)
        kept = gz.at[j // 3, pl.ds(j % 3 * TOK, TOK)]
        for k in range(2):
            width = SLICE // 2
            rows = xr[pl.ds(0, EARLY), :, pl.ds(j * SLICE + k * width, width)].reshape(EARLY * CAP, width)
            kept[:, pl.ds(k * width, width)] = tn(put[pl.ds(0, EARLY * CAP), :], rows).astype(bf)
        early_out.append(pltpu.make_async_copy(kept, early_h.at[:, cols], early_sem.at[j]))
        early_out[-1].start()

    wait_recv(dn_in, dn_recv)
    for j in range(2):
        own += dn_in[j].astype(f32)
    out_d[...] = own.astype(bf)
    down_out = pltpu.make_async_copy(out_d, down_h, out_sem.at[1])
    down_out.start()

    most = pl.ds(0, NE - 1)
    wait_send(sx.at[most], x_send)
    wait_send(sdy.at[most], dy_send)
    wait_send(tokdy.at[:, :, pl.ds(0, (NZ - 1) * SLICE)], dn_send)
    wait_send(pg.at[most], pg_send)
    wait_send(pc.at[most], pc_send)
    for copy in give_back(OWN):
        copy.wait()
    wait_recv(back_c.at[most], pc_recv)
    sums = back_c[...].reshape(NE * CAP, 128)
    for k, rows in ((0, put0), (1, put1)):
        both = tn(sums, rows[...])
        out_c[k : k + 1, :] = (both[0:1] + both[64:65]) / weight_t[k : k + 1, :].astype(f32)
    wait_recv(back.at[pl.ds(EARLY, GROUP - 1)], pg_recv.at[GROUPS - 1])
    for copy in early_out:
        copy.wait()
    wide_out.wait()
    down_out.wait()


def exchange(ids_t, weight_t, tokens, grad_out, w_gate, w_up, w_down):
    bf, f32 = jnp.bfloat16, jnp.float32
    any_ = pl.BlockSpec(memory_space=pl.ANY)
    vm = pl.BlockSpec(memory_space=pltpu.VMEM)
    dma = pltpu.SemaphoreType.DMA
    return pl.pallas_call(
        kernel,
        out_shape=(
            jax.ShapeDtypeStruct((NE, CAP, D), bf),
            jax.ShapeDtypeStruct((NE, CAP, D), bf),
            jax.ShapeDtypeStruct((NE, CAP, D), bf),
            jax.ShapeDtypeStruct((TOK, D), bf),
            jax.ShapeDtypeStruct((ROWS, TOK), bf),
            jax.ShapeDtypeStruct((2, TOK), f32),
            jax.ShapeDtypeStruct((SLICE, 2 * HID), bf),
            jax.ShapeDtypeStruct((HID, SLICE), bf),
        ),
        in_specs=[vm] * 2 + [any_] * 5,
        out_specs=(any_, any_, any_, any_, vm, vm, any_, any_),
        scratch_shapes=[
            pltpu.VMEM((2, TOK, D), bf),
            pltpu.VMEM((D // SC, GROUP, CAP, SC), bf),
            pltpu.VMEM((SLICE, 2 * HID), bf),
            pltpu.VMEM((HID, SLICE), bf),
            pltpu.VMEM((NE * CAP, TOK), bf),
            pltpu.VMEM((NE * CAP, TOK), bf),
            pltpu.VMEM((NE * CAP, TOK), bf),
            pltpu.VMEM((NE * CAP, TOK), bf),
            pltpu.VMEM((NE, CAP, 128), bf),
            pltpu.VMEM((NE, CAP, D), bf),
            pltpu.VMEM((NE, CAP, D), bf),
            pltpu.VMEM((NE, CAP, D), bf),
            pltpu.VMEM((NE, CAP, 128), bf),
            pltpu.VMEM((D, HID), bf),
            pltpu.VMEM((D, HID), bf),
            pltpu.VMEM((HID, D), bf),
            pltpu.VMEM((NZ - 1, NE, CAP, SLICE), bf),
            pltpu.VMEM((NZ - 1, NE * CAP, 2 * HID), bf),
            pltpu.VMEM((NE * CAP, 2 * HID), bf),
            pltpu.VMEM((NE * CAP, HID), bf),
            pltpu.VMEM((2, HID, SLICE), bf),
            pltpu.VMEM((2, HID // 2, SLICE), bf),
            pltpu.VMEM((ROWS, HID), f32),
            pltpu.VMEM((ROWS, HID), f32),
            dma((2,)), dma((2,)), dma((D // SLICE,)), dma((2,)), dma((3,)), dma((4,)), dma((GROUPS,)), dma((GROUPS,)),
        ] + [dma, dma, dma((GROUPS,)), dma, dma, dma] + [dma] * 2 + [dma((GROUPS,)), dma((GROUPS,)), dma, dma, dma, dma((2,)), dma],
        compiler_params=pltpu.CompilerParams(
            collective_id=0, has_side_effects=True, vmem_limit_bytes=VMEM_BYTES
        ),
    )(ids_t, weight_t, tokens, grad_out, w_gate, w_up, w_down)


def finish_kernel(
    put_last, sums, early, back, wide, down, grad_tokens, grad_combine, grad_gate, grad_up, grad_down,
    rows, made, wide_v, down_v, load_sem, out_sem,
):
    steps = 4
    width = D // steps
    cols = [pl.ds(k * width, width) for k in range(steps)]
    last = pl.ds(EARLY, GROUP)
    loads = [pltpu.make_async_copy(back.at[last, :, kk], rows.at[:, :, kk], load_sem.at[k]) for k, kk in enumerate(cols)]
    firsts = [pltpu.make_async_copy(early.at[:, kk], made.at[:, kk], load_sem.at[steps + k]) for k, kk in enumerate(cols)]
    loads.append(pltpu.make_async_copy(wide, wide_v, load_sem.at[2 * steps]))
    loads.append(pltpu.make_async_copy(down, down_v, load_sem.at[2 * steps + 1]))
    for pair in zip(loads, firsts):
        for copy in pair:
            copy.start()
    for copy in loads[steps:]:
        copy.start()
    moves = []
    grad_combine[...] = sums[...].astype(jnp.bfloat16)
    for k, kk in enumerate(cols):
        loads[k].wait()
        firsts[k].wait()
        block = rows[:, :, kk].reshape(ROWS, width)
        made[:, kk] = (made[:, kk].astype(jnp.float32) + tn(put_last[...], block)).astype(jnp.bfloat16)
        moves.append(pltpu.make_async_copy(made.at[:, kk], grad_tokens.at[:, kk], out_sem.at[3 + k]))
        moves[-1].start()
    loads[steps].wait()
    loads[steps + 1].wait()
    for src, dst, sem in (
        (wide_v.at[:, pl.ds(0, HID)], grad_gate, 0), (wide_v.at[:, pl.ds(HID, HID)], grad_up, 1), (down_v, grad_down, 2),
    ):
        moves.append(pltpu.make_async_copy(src, dst, out_sem.at[sem]))
        moves[-1].start()
    for copy in moves:
        copy.wait()


def finish(put_last, sums, early, back, wide, down):
    bf = jnp.bfloat16
    any_ = pl.BlockSpec(memory_space=pl.ANY)
    vm = pl.BlockSpec(memory_space=pltpu.VMEM)
    return pl.pallas_call(
        finish_kernel,
        out_shape=(
            jax.ShapeDtypeStruct((TOK, D), bf),
            jax.ShapeDtypeStruct((2, TOK), bf),
            jax.ShapeDtypeStruct((SLICE, HID), bf),
            jax.ShapeDtypeStruct((SLICE, HID), bf),
            jax.ShapeDtypeStruct((HID, SLICE), bf),
        ),
        in_specs=[vm, vm, any_, any_, any_, any_],
        out_specs=(any_, vm, any_, any_, any_),
        scratch_shapes=[
            pltpu.VMEM((GROUP, CAP, D), bf),
            pltpu.VMEM((TOK, D), bf),
            pltpu.VMEM((SLICE, 2 * HID), bf),
            pltpu.VMEM((HID, SLICE), bf),
            pltpu.SemaphoreType.DMA((10,)),
            pltpu.SemaphoreType.DMA((7,)),
        ],
        compiler_params=pltpu.CompilerParams(vmem_limit_bytes=60 * 2**20),
    )(put_last, sums, early, back, wide, down)


def on_device(tokens, grad_out, expert_ids, combine, w_gate, w_up, w_down):
    back, _, _, early, put_last, sums, wide, down = exchange(
        expert_ids.T, combine.T, tokens, grad_out, w_gate[0], w_up[0], w_down[0]
    )
    grad_tokens, grad_combine, grad_gate, grad_up, grad_down = finish(put_last, sums, early, back, wide, down)
    return grad_tokens, grad_combine.T, grad_gate[None], grad_up[None], grad_down[None]


def solution(mesh):
    return jax.shard_map(
        on_device,
        mesh=mesh,
        in_specs=(
            P(("dp", "expert"), None),
            P(("dp", "expert"), None),
            P(("dp", "expert"), None),
            P(("dp", "expert"), None),
            P("expert", None, None),
            P("expert", None, None),
            P("expert", None, None),
        ),
        out_specs=(
            P(("dp", "expert"), None),
            P(("dp", "expert"), None),
            P("expert", "dp", None),
            P("expert", "dp", None),
            P("expert", None, "dp"),
        ),
        check_vma=False,
    )
```

```python
import jax
import jax.numpy as jnp
from jax import lax
from jax.experimental import pallas as pl
from jax.experimental.pallas import tpu as pltpu
from jax.sharding import PartitionSpec as P

MESH = pl.DeviceIdType.MESH
NX, NY, NZ, NE = 4, 4, 4, 32
CAP = 24
D, HID = 4096, 512
SLICE = D // NZ
GROUP = 8
GROUPS = NE // GROUP
ROWS = GROUP * CAP
EARLY = NE - GROUP
TOK = 256
PARTNER, OWN = NE - 2, NE - 1
SC = 2048
VMEM_BYTES = 63 * 2**20
OFFSETS = (
    (1, 0), (3, 0), (0, 1), (0, 3), (1, 1), (3, 3), (1, 3), (3, 1),
    (2, 0), (0, 2), (1, 2), (3, 2), (2, 1), (2, 3), (2, 2),
)


def offset(i, core):
    dx, dy = OFFSETS[i]
    return dx + core * (dy - dx), dy + core * (dx - dy)


def expert_at(x, y, core):
    return (y % NY) * (2 * NX) + (x % NX) * 2 + core


def nt(left, right):
    return lax.dot_general(left, right, (((1,), (1,)), ((), ())), preferred_element_type=jnp.float32)


def tn(left, right):
    return lax.dot_general(left, right, (((0,), (0,)), ((), ())), preferred_element_type=jnp.float32)


def kernel(
    ids_t, weight_t, tok_h, dy_h, wg_h, wu_h, wd_h,
    back, sx, sdy, early_h, put_last, out_c, wide_h, down_h,
    tokdy, stage, out_gu, out_d, put, put0, put1, put_dy, back_c, xr, dyr, pg, pc, wg, wu, wd, xz, gz, gown, hid, dn_in, dn_rel, fa, fb,
    in_sem, out_sem, early_sem, st_sem, w_sem, loc_sem, x_recv, dy_recv, x_send, dy_send, pg_recv, pg_send, pc_recv, pc_send,
    xz_recv, xz_send, gz_next, gz_prev, gz_far, gz_send, dn_recv, rel_recv, dn_send,
):
    bf, f32 = jnp.bfloat16, jnp.float32
    z = lax.axis_index("dp")
    ex = lax.axis_index("expert")
    c = ex % 2
    x = (ex // 2) % NX
    y = ex // (2 * NX)

    loads = [
        pltpu.make_async_copy(wg_h, wg, w_sem.at[0]),
        pltpu.make_async_copy(wu_h, wu, w_sem.at[1]),
        pltpu.make_async_copy(wd_h, wd, w_sem.at[2]),
        pltpu.make_async_copy(sx.at[OWN], xr.at[OWN], loc_sem.at[0]),
        pltpu.make_async_copy(sdy.at[OWN], dyr.at[OWN], loc_sem.at[1]),
    ]

    barrier = pltpu.get_barrier_semaphore()

    def greet(k, carry):
        pl.semaphore_signal(barrier, inc=1, device_id=(z, (ex + k) % NE), device_id_type=MESH)
        return carry

    lax.fori_loop(1, NE, greet, 0)
    for j in range(1, NZ):
        pl.semaphore_signal(barrier, inc=1, device_id=((z + j) % NZ, ex), device_id_type=MESH)
    fetch = [pltpu.make_async_copy(tok_h, tokdy.at[0], in_sem.at[0]), pltpu.make_async_copy(dy_h, tokdy.at[1], in_sem.at[1])]
    for load in fetch + loads[:3]:
        load.start()

    ids = [ids_t[k : k + 1, :].astype(f32) for k in range(2)]
    weight = weight_t[...].astype(f32)
    position = lax.broadcasted_iota(jnp.int32, (NE, TOK), 0)
    label = jnp.where(position == OWN, ex, ex + 1 - 2 * c)
    for n in range(PARTNER):
        dx, dy = offset(n // 2, c)
        label = jnp.where(position == n, expert_at(x + dx, y + dy, n % 2), label)
    label = label.astype(f32)
    position = position.astype(f32)
    hits = [(label == ids[k]).astype(f32) for k in range(2)]
    first = lax.broadcasted_iota(jnp.int32, (TOK, TOK), 0)
    second = lax.broadcasted_iota(jnp.int32, (TOK, TOK), 1)
    before = (first < second).astype(f32).astype(bf)
    earlier = jnp.dot((hits[0] + hits[1]).astype(bf), before, preferred_element_type=f32)
    places = [jnp.sum((position * CAP + earlier) * hits[k], axis=0, keepdims=True) for k in range(2)]
    index = lax.broadcasted_iota(jnp.int32, (NE * CAP, TOK), 0).astype(f32)
    put_k = [(index == places[k]).astype(f32) for k in range(2)]
    put[...] = (put_k[0] + put_k[1]).astype(bf)
    put0[...] = put_k[0].astype(bf)
    put1[...] = put_k[1].astype(bf)
    put_dy[...] = (put_k[0] * weight[0:1] + put_k[1] * weight[1:2]).astype(bf)

    def to_expert(src, dst, send, recv, n):
        if n == PARTNER:
            to, slot = ex + 1 - 2 * c, PARTNER
        else:
            i, core = n // 2, n % 2
            dx, dy = offset(i, c)
            to, slot = expert_at(x + dx, y + dy, core), 2 * i + c
        return pltpu.make_async_remote_copy(
            src_ref=src.at[n], dst_ref=dst.at[slot], send_sem=send, recv_sem=recv.at[n // GROUP],
            device_id=(z, to), device_id_type=MESH,
        )

    kinds = ((put, sx, xr, x_send, x_recv), (put_dy, sdy, dyr, dy_send, dy_recv))

    def stage_out(step, h):
        which, g = divmod(step, GROUPS)
        kk = pl.ds(pl.multiple_of(h * SC, SC), SC)
        return pltpu.make_async_copy(
            stage.at[h], kinds[which][1].at[pl.ds(GROUP * g, GROUP), :, kk], st_sem.at[h]
        )

    def leave(step):
        which, g = divmod(step, GROUPS)
        _, src, dst, send, recv = kinds[which]
        for n in range(GROUP * g, GROUP * (g + 1)):
            if n == OWN:
                loads[3 + which].start()
            else:
                to_expert(src, dst, send, recv, n).start()

    for step in range(2 * GROUPS):
        which, g = divmod(step, GROUPS)
        if g == 0:
            fetch[which].wait()

        def lay_out(h, carry):
            if step > 0:
                stage_out(step - 1, h).wait()
            kk = pl.ds(pl.multiple_of(h * SC, SC), SC)
            made = jnp.dot(kinds[which][0][pl.ds(g * ROWS, ROWS), :], tokdy[which, :, kk], preferred_element_type=f32)
            stage[h] = made.reshape(GROUP, CAP, SC).astype(bf)
            stage_out(step, h).start()
            return carry

        lax.fori_loop(0, D // SC, lay_out, 0)
        if step == 1:
            pl.semaphore_wait(barrier, NE - 1 + NZ - 1)
        if step > 0:
            leave(step - 1)
    for h in range(D // SC):
        stage_out(2 * GROUPS - 1, h).wait()
    leave(2 * GROUPS - 1)

    def wait_recv(dst, sem):
        pltpu.make_async_remote_copy(
            src_ref=dst, dst_ref=dst, send_sem=x_send, recv_sem=sem,
            device_id=(z, (ex + 1) % NE), device_id_type=MESH,
        ).wait_recv()

    def wait_send(src, sem):
        pltpu.make_async_remote_copy(
            src_ref=src, dst_ref=src, send_sem=sem, recv_sem=x_recv.at[0],
            device_id=(z, (ex + 1) % NE), device_id_type=MESH,
        ).wait_send()

    def arrive(dst, recv, own, g):
        @pl.when(g == GROUPS - 1)
        def _():
            loads[own].wait()
            wait_recv(dst.at[pl.ds(NE - GROUP, GROUP - 1)], recv.at[GROUPS - 1])

        @pl.when(g < GROUPS - 1)
        def _():
            wait_recv(dst.at[pl.ds(GROUP * g, GROUP)], recv.at[g])

    def over_z(src, dst, send, recv, j):
        return pltpu.make_async_remote_copy(
            src_ref=src, dst_ref=dst, send_sem=send, recv_sem=recv,
            device_id=((z + j) % NZ, ex), device_id_type=MESH,
        )

    def give_back(slot):
        if slot == OWN:
            return [
                pltpu.make_async_copy(pg.at[OWN], back.at[OWN], loc_sem.at[2]),
                pltpu.make_async_copy(pc.at[OWN], back_c.at[OWN], loc_sem.at[3]),
            ]
        if slot == PARTNER:
            to, n = ex + 1 - 2 * c, PARTNER
        else:
            i, core = slot // 2, slot % 2
            dx, dy = offset(i, core)
            to, n = expert_at(x - dx, y - dy, core), 2 * i + c
        return [
            pltpu.make_async_remote_copy(
                src_ref=src.at[slot], dst_ref=dst.at[n], send_sem=send, recv_sem=recv,
                device_id=(z, to), device_id_type=MESH,
            )
            for src, dst, send, recv in ((pg, back, pg_send, pg_recv.at[slot // GROUP]), (pc, back_c, pc_send, pc_recv))
        ]

    put_last[...] = put[pl.ds(EARLY * CAP, ROWS), :]

    for load in loads[:3]:
        load.wait()

    def pass_on(g):
        rows = pl.ds(pl.multiple_of(g * ROWS, ROWS), ROWS)
        wait_recv(gz.at[0, rows], gz_next.at[g])
        low = pl.ds(pl.multiple_of(g * ROWS, ROWS // 2), ROWS // 2)
        over_z(gz.at[0, low], gz.at[1, low], gz_send, gz_far, 1).start()
        wait_recv(gz.at[2, rows], gz_prev.at[g])
        high = pl.ds(pl.multiple_of(g * ROWS + ROWS // 2, ROWS // 2), ROWS // 2)
        over_z(gz.at[2, high], gz.at[1, high], gz_send, gz_far, 3).start()

    def spread(g, carry):
        base = pl.multiple_of(GROUP * g, GROUP)
        arrive(xr, x_recv, 3, g)
        for j in (2, 1, 3):
            cols = pl.ds(pl.multiple_of((z + j) % NZ * SLICE, SLICE), SLICE)
            over_z(xr.at[pl.ds(base, GROUP), :, cols], xz.at[j - 1, pl.ds(base, GROUP)], xz_send, xz_recv, j).start()
        return carry

    lax.fori_loop(0, GROUPS, spread, 0)

    KC = 1024

    def group_step(g, carry):
        base = pl.multiple_of(GROUP * g, GROUP)
        rows = pl.ds(pl.multiple_of(g * ROWS, ROWS), ROWS)
        fa[...] = jnp.zeros_like(fa)
        fb[...] = jnp.zeros_like(fb)

        def forward(k, cc):
            kk = pl.ds(pl.multiple_of(k * KC, KC), KC)
            xk = xr[pl.ds(base, GROUP), :, kk].reshape(ROWS, KC)
            fa[...] += jnp.dot(xk, wg[kk, :], preferred_element_type=jnp.float32)
            fb[...] += jnp.dot(xk, wu[kk, :], preferred_element_type=jnp.float32)
            return cc

        lax.fori_loop(0, D // KC, forward, 0)
        gate = fa[...]
        upper = fb[...]
        sigma = 1.0 / (1.0 + jnp.exp(-gate))
        swish = gate * sigma
        hidden = (swish * upper).astype(jnp.bfloat16)
        hid[rows, :] = hidden
        fa[...] = upper * sigma * (1.0 + gate * (1.0 - sigma))
        fb[...] = swish

        @pl.when(g >= 1)
        def _():
            pass_on(g - 1)

        arrive(dyr, dy_recv, 4, g)

        def backward(k, hg):
            kk = pl.ds(pl.multiple_of(k * KC, KC), KC)
            dk = dyr[pl.ds(base, GROUP), :, kk].reshape(ROWS, KC)
            return hg + nt(dk, wd[:, kk])

        hg = lax.fori_loop(0, D // KC, backward, jnp.zeros((ROWS, HID), jnp.float32))
        gown[rows, pl.ds(0, HID)] = (hg * fa[...]).astype(jnp.bfloat16)
        gown[rows, pl.ds(HID, HID)] = (hg * fb[...]).astype(jnp.bfloat16)
        over_z(gown.at[rows], gz.at[0, rows], gz_send, gz_next.at[g], 1).start()
        over_z(gown.at[rows], gz.at[2, rows], gz_send, gz_prev.at[g], 3).start()
        total = jnp.sum(hid[rows, :].astype(jnp.float32) * hg, axis=1, keepdims=True)
        total = jnp.broadcast_to(total, (ROWS, 128))
        high = total.astype(jnp.bfloat16).astype(jnp.float32)
        lane = lax.broadcasted_iota(jnp.int32, (ROWS, 128), 1)
        pc[pl.ds(base, GROUP)] = (
            jnp.where(lane < 64, high, total - high).reshape(GROUP, CAP, 128).astype(jnp.bfloat16)
        )

        def inward(k, cc):
            kk = pl.ds(pl.multiple_of(k * KC, KC), KC)
            part = nt(gown[rows, pl.ds(0, HID)], wg[kk, :]) + nt(gown[rows, pl.ds(HID, HID)], wu[kk, :])
            pg[pl.ds(base, GROUP), :, kk] = part.reshape(GROUP, CAP, KC).astype(jnp.bfloat16)
            return cc

        lax.fori_loop(0, D // KC, inward, 0)
        for done in range(GROUPS):

            @pl.when(g == done)
            def _():
                for slot in range(GROUP * done, GROUP * (done + 1)):
                    for copy in give_back(slot):
                        copy.start()

        return carry

    lax.fori_loop(0, GROUPS, group_step, 0)

    pass_on(GROUPS - 1)

    def down_part(j):
        cols = pl.ds(pl.multiple_of((z + j) % NZ * SLICE, SLICE), SLICE)
        total = jnp.zeros((HID, SLICE), jnp.float32)

        def add(g, total):
            rows = pl.ds(pl.multiple_of(g * ROWS, ROWS), ROWS)
            dk = dyr[pl.ds(pl.multiple_of(GROUP * g, GROUP), GROUP), :, cols].reshape(ROWS, SLICE)
            return total + tn(hid[rows, :], dk)

        return lax.fori_loop(0, GROUPS, add, total)

    half = HID // 2
    low, high = pl.ds(0, half), pl.ds(half, half)

    def dn_out(h, j):
        return tokdy.at[h, :, pl.ds((j - 1) * SLICE, SLICE)]

    def make_down(j):
        part = down_part(j).astype(bf)
        dn_out(0, j)[...] = part[:half]
        dn_out(1, j)[...] = part[half:]

    make_down(2)
    over_z(dn_out(0, 2), dn_rel.at[0], dn_send, rel_recv.at[0], 1).start()
    over_z(dn_out(1, 2), dn_rel.at[1], dn_send, rel_recv.at[1], 3).start()
    make_down(1)
    over_z(dn_out(1, 1), dn_in.at[0, high], dn_send, dn_recv, 1).start()
    make_down(3)
    over_z(dn_out(0, 3), dn_in.at[1, low], dn_send, dn_recv, 3).start()

    wait_recv(xz, xz_recv)
    wait_recv(gz.at[1], gz_far)
    CB = 256

    def wide(k, carry):
        off = pl.multiple_of(k * CB, CB)
        mine = pl.ds(pl.multiple_of(z * SLICE + off, CB), CB)
        total = tn(xr[:, :, mine].reshape(NE * CAP, CB), gown[...])
        for j in range(NZ - 1):
            total += tn(xz[j, :, :, pl.ds(off, CB)].reshape(NE * CAP, CB), gz[j])
        out_gu[pl.ds(off, CB), :] = total.astype(bf)
        return carry

    lax.fori_loop(0, SLICE // CB, wide, 0)
    wide_out = pltpu.make_async_copy(out_gu, wide_h, out_sem.at[0])
    wide_out.start()

    for h, j in ((0, 1), (1, 3)):
        wait_recv(dn_rel.at[h], rel_recv.at[h])
        dn_out(h, j)[...] = (dn_out(h, j)[...].astype(f32) + dn_rel[h].astype(f32)).astype(bf)
        over_z(dn_out(h, j), dn_in.at[h, high if h else low], dn_send, dn_recv, j).start()
    own = down_part(0)

    wait_send(xz, xz_send)
    wait_send(gz, gz_send)
    for g in range(GROUPS - 1):
        part = pl.ds(GROUP * g, GROUP)
        wait_recv(back.at[part], pg_recv.at[g])
        pltpu.make_async_copy(back.at[part], xr.at[part], st_sem.at[0]).start()
        pltpu.make_async_copy(back.at[part], xr.at[part], st_sem.at[0]).wait()
    early_out = []
    for j in range(D // SLICE):
        cols = pl.ds(j * SLICE, SLICE)
        kept = gz.at[j // 3, pl.ds(j % 3 * TOK, TOK)]
        for k in range(2):
            width = SLICE // 2
            rows = xr[pl.ds(0, EARLY), :, pl.ds(j * SLICE + k * width, width)].reshape(EARLY * CAP, width)
            kept[:, pl.ds(k * width, width)] = tn(put[pl.ds(0, EARLY * CAP), :], rows).astype(bf)
        early_out.append(pltpu.make_async_copy(kept, early_h.at[:, cols], early_sem.at[j]))
        early_out[-1].start()

    wait_recv(dn_in, dn_recv)
    for j in range(2):
        own += dn_in[j].astype(f32)
    out_d[...] = own.astype(bf)
    down_out = pltpu.make_async_copy(out_d, down_h, out_sem.at[1])
    down_out.start()

    most = pl.ds(0, NE - 1)
    wait_send(sx.at[most], x_send)
    wait_send(sdy.at[most], dy_send)
    wait_send(tokdy.at[:, :, pl.ds(0, (NZ - 1) * SLICE)], dn_send)
    wait_send(pg.at[most], pg_send)
    wait_send(pc.at[most], pc_send)
    for copy in give_back(OWN):
        copy.wait()
    wait_recv(back_c.at[most], pc_recv)
    sums = back_c[...].reshape(NE * CAP, 128)
    weight = weight_t[...].astype(f32)
    for k, rows in ((0, put0), (1, put1)):
        both = tn(sums, rows[...])
        out_c[k : k + 1, :] = (both[0:1] + both[64:65]) / weight[k : k + 1]
    wait_recv(back.at[pl.ds(EARLY, GROUP - 1)], pg_recv.at[GROUPS - 1])
    for copy in early_out:
        copy.wait()
    wide_out.wait()
    down_out.wait()


def exchange(ids_t, weight_t, tokens, grad_out, w_gate, w_up, w_down):
    bf, f32 = jnp.bfloat16, jnp.float32
    any_ = pl.BlockSpec(memory_space=pl.ANY)
    vm = pl.BlockSpec(memory_space=pltpu.VMEM)
    dma = pltpu.SemaphoreType.DMA
    return pl.pallas_call(
        kernel,
        out_shape=(
            jax.ShapeDtypeStruct((NE, CAP, D), bf),
            jax.ShapeDtypeStruct((NE, CAP, D), bf),
            jax.ShapeDtypeStruct((NE, CAP, D), bf),
            jax.ShapeDtypeStruct((TOK, D), bf),
            jax.ShapeDtypeStruct((ROWS, TOK), bf),
            jax.ShapeDtypeStruct((2, TOK), f32),
            jax.ShapeDtypeStruct((SLICE, 2 * HID), bf),
            jax.ShapeDtypeStruct((HID, SLICE), bf),
        ),
        in_specs=[vm] * 2 + [any_] * 5,
        out_specs=(any_, any_, any_, any_, vm, vm, any_, any_),
        scratch_shapes=[
            pltpu.VMEM((2, TOK, D), bf),
            pltpu.VMEM((D // SC, GROUP, CAP, SC), bf),
            pltpu.VMEM((SLICE, 2 * HID), bf),
            pltpu.VMEM((HID, SLICE), bf),
            pltpu.VMEM((NE * CAP, TOK), bf),
            pltpu.VMEM((NE * CAP, TOK), bf),
            pltpu.VMEM((NE * CAP, TOK), bf),
            pltpu.VMEM((NE * CAP, TOK), bf),
            pltpu.VMEM((NE, CAP, 128), bf),
            pltpu.VMEM((NE, CAP, D), bf),
            pltpu.VMEM((NE, CAP, D), bf),
            pltpu.VMEM((NE, CAP, D), bf),
            pltpu.VMEM((NE, CAP, 128), bf),
            pltpu.VMEM((D, HID), bf),
            pltpu.VMEM((D, HID), bf),
            pltpu.VMEM((HID, D), bf),
            pltpu.VMEM((NZ - 1, NE, CAP, SLICE), bf),
            pltpu.VMEM((NZ - 1, NE * CAP, 2 * HID), bf),
            pltpu.VMEM((NE * CAP, 2 * HID), bf),
            pltpu.VMEM((NE * CAP, HID), bf),
            pltpu.VMEM((2, HID, SLICE), bf),
            pltpu.VMEM((2, HID // 2, SLICE), bf),
            pltpu.VMEM((ROWS, HID), f32),
            pltpu.VMEM((ROWS, HID), f32),
            dma((2,)), dma((2,)), dma((D // SLICE,)), dma((2,)), dma((3,)), dma((4,)), dma((GROUPS,)), dma((GROUPS,)),
        ] + [dma, dma, dma((GROUPS,)), dma, dma, dma] + [dma] * 2 + [dma((GROUPS,)), dma((GROUPS,)), dma, dma, dma, dma((2,)), dma],
        compiler_params=pltpu.CompilerParams(
            collective_id=0, has_side_effects=True, vmem_limit_bytes=VMEM_BYTES
        ),
    )(ids_t, weight_t, tokens, grad_out, w_gate, w_up, w_down)


def finish_kernel(
    put_last, sums, early, back, wide, down, grad_tokens, grad_combine, grad_gate, grad_up, grad_down,
    rows, made, wide_v, down_v, put_v, load_sem, out_sem,
):
    steps = 4
    width = D // steps
    cols = [pl.ds(k * width, width) for k in range(steps)]
    last = pl.ds(EARLY, GROUP)
    loads = [pltpu.make_async_copy(back.at[last, :, kk], rows.at[:, :, kk], load_sem.at[k]) for k, kk in enumerate(cols)]
    firsts = [pltpu.make_async_copy(early.at[:, kk], made.at[:, kk], load_sem.at[steps + k]) for k, kk in enumerate(cols)]
    loads.append(pltpu.make_async_copy(wide, wide_v, load_sem.at[2 * steps]))
    loads.append(pltpu.make_async_copy(down, down_v, load_sem.at[2 * steps + 1]))
    put_in = pltpu.make_async_copy(put_last, put_v, load_sem.at[2 * steps + 2])
    put_in.start()
    for pair in zip(loads, firsts):
        for copy in pair:
            copy.start()
    for copy in loads[steps:]:
        copy.start()
    moves = []
    grad_combine[...] = sums[...].astype(jnp.bfloat16)
    put_in.wait()
    for k, kk in enumerate(cols):
        loads[k].wait()
        firsts[k].wait()
        block = rows[:, :, kk].reshape(ROWS, width)
        made[:, kk] = (made[:, kk].astype(jnp.float32) + tn(put_v[...], block)).astype(jnp.bfloat16)
        moves.append(pltpu.make_async_copy(made.at[:, kk], grad_tokens.at[:, kk], out_sem.at[3 + k]))
        moves[-1].start()
    loads[steps].wait()
    loads[steps + 1].wait()
    for src, dst, sem in (
        (wide_v.at[:, pl.ds(0, HID)], grad_gate, 0), (wide_v.at[:, pl.ds(HID, HID)], grad_up, 1), (down_v, grad_down, 2),
    ):
        moves.append(pltpu.make_async_copy(src, dst, out_sem.at[sem]))
        moves[-1].start()
    for copy in moves:
        copy.wait()


def finish(put_last, sums, early, back, wide, down):
    bf = jnp.bfloat16
    any_ = pl.BlockSpec(memory_space=pl.ANY)
    vm = pl.BlockSpec(memory_space=pltpu.VMEM)
    return pl.pallas_call(
        finish_kernel,
        out_shape=(
            jax.ShapeDtypeStruct((TOK, D), bf),
            jax.ShapeDtypeStruct((2, TOK), bf),
            jax.ShapeDtypeStruct((SLICE, HID), bf),
            jax.ShapeDtypeStruct((SLICE, HID), bf),
            jax.ShapeDtypeStruct((HID, SLICE), bf),
        ),
        in_specs=[any_, vm, any_, any_, any_, any_],
        out_specs=(any_, vm, any_, any_, any_),
        scratch_shapes=[
            pltpu.VMEM((GROUP, CAP, D), bf),
            pltpu.VMEM((TOK, D), bf),
            pltpu.VMEM((SLICE, 2 * HID), bf),
            pltpu.VMEM((HID, SLICE), bf),
            pltpu.VMEM((ROWS, TOK), bf),
            pltpu.SemaphoreType.DMA((11,)),
            pltpu.SemaphoreType.DMA((7,)),
        ],
        compiler_params=pltpu.CompilerParams(vmem_limit_bytes=60 * 2**20),
    )(put_last, sums, early, back, wide, down)


def on_device(tokens, grad_out, expert_ids, combine, w_gate, w_up, w_down):
    back, _, _, early, put_last, sums, wide, down = exchange(
        expert_ids.T, combine.T, tokens, grad_out, w_gate[0], w_up[0], w_down[0]
    )
    grad_tokens, grad_combine, grad_gate, grad_up, grad_down = finish(put_last, sums, early, back, wide, down)
    return grad_tokens, grad_combine.T, grad_gate[None], grad_up[None], grad_down[None]


def solution(mesh):
    return jax.shard_map(
        on_device,
        mesh=mesh,
        in_specs=(
            P(("dp", "expert"), None),
            P(("dp", "expert"), None),
            P(("dp", "expert"), None),
            P(("dp", "expert"), None),
            P("expert", None, None),
            P("expert", None, None),
            P("expert", None, None),
        ),
        out_specs=(
            P(("dp", "expert"), None),
            P(("dp", "expert"), None),
            P("expert", "dp", None),
            P("expert", "dp", None),
            P("expert", None, "dp"),
        ),
        check_vma=False,
    )
```
